512 devices in a mesh: blk: 128 (over y, x_lo, z), quad: 4 (over x_hi, core).
Axes of the slice: x: 4 (x_hi: 2, x_lo: 2; x = x_hi * 2 + x_lo), y: 4, z: 16, core: 2. Of those that a mesh axis runs over, the one named last changes fastest.
Arguments:
- positions: float32 [3, 16384], P(None, ('blk', 'quad')), may hold values from 0 to 1
- forces: float32 [3, 16, 16384], P(None, None, ('blk', 'quad')), may hold values from -6 to 6
Outputs:
- velocity: float32 [3, 16, 16384], P(None, None, ('blk', 'quad'))
The draws below stay inside these ranges and needn't reach their ends.
All inputs are finite; a program needn't handle non-finite values.
Results may differ from the reference program's by a relative error of at most 0.0003.
Values sent between devices are 32-bit elements; how exact they have to be, the bound alone decides.
A program may use at most 64 MiB of HBM per device.

```python
import math
import jax
import jax.numpy as jnp
from jax import lax

VEC = 16
BLOBS = 16384


def steps_of(stream_key, dims, pieces, smallest, high):
    def one(dim, blocks):
        steps = jax.random.uniform(jax.random.fold_in(jax.random.fold_in(stream_key, 6), dim), (blocks,), jnp.float32, smallest / len(pieces), high / len(pieces))
        return jnp.repeat(jnp.exp(steps), dims[dim] // blocks).reshape((-1,) + (1,) * (len(dims) - dim - 1))

    loudness = one(*pieces[0])
    for cut in pieces[1:]:
        loudness = loudness * one(*cut)
    return loudness


def normal_values(rng, extent, width, bound, pieces=(), held_as=jnp.bfloat16):
    entries = width * jax.random.normal(rng, extent, jnp.float32)
    if pieces:
        entries = entries * steps_of(rng, extent, pieces, -0.22, 0.18)
    return jnp.clip(entries, -bound, bound).astype(held_as)


def setup_inputs(seed: int = 0) -> dict:
    seeds = jax.random.split(jax.random.key(seed), 3)
    return {
        "positions": jnp.clip(1.0 * jax.random.uniform(seeds[0], (3, BLOBS), jnp.float32) ** steps_of(seeds[0], (3, BLOBS), ((1, 512),), -0.2, 0.2), 0.0, 1.0),
        "forces": normal_values(seeds[1], (3, VEC, BLOBS), 1.0, 6.0, ((2, 512),), jnp.float32),
    }


radius_scale = 0.3

def mobility_tile(home_pos, visit_pos, radius):
    separation = home_pos[:, :, None] - visit_pos[:, None, :]
    squared = lax.optimization_barrier(jnp.sum(separation * separation, axis=0))
    distance = jnp.sqrt(squared)
    far_dist = jnp.maximum(distance, 2.0 * radius)
    inverse = 1.0 / far_dist
    ratio_sq = radius * radius * inverse * inverse
    factor = 0.75 * radius * inverse
    iso_far = factor * (1.0 + 2.0 / 3.0 * ratio_sq)
    dyad_far = factor * (1.0 - 2.0 * ratio_sq) * inverse * inverse
    iso_near = 1.0 - 9.0 / 32.0 * distance / radius
    dyad_near = 3.0 / 32.0 / (radius * jnp.maximum(distance, radius / 1000.0))
    near_mask = distance < 2.0 * radius
    coef_iso = jnp.where(near_mask, iso_near, iso_far)
    coef_dyad = jnp.where(near_mask, dyad_near, dyad_far)
    identity = jnp.eye(3, dtype=jnp.float32)
    return coef_dyad[None, None] * separation[:, None] * separation[None, :] + identity[:, :, None, None] * coef_iso[None, None]

def reference(positions, forces):
    total = positions.shape[1]
    radius = radius_scale / total ** (1.0 / 3.0)
    home_rows = math.gcd(total, 512)
    col_rows = math.gcd(total, 2048)

    def one_home(home_start):
        home_pos = lax.dynamic_slice_in_dim(positions, home_start, home_rows, 1)

        def one_col(accum, col_start):
            col_pos = lax.dynamic_slice_in_dim(positions, col_start, col_rows, 1)
            col_force = lax.dynamic_slice_in_dim(forces, col_start, col_rows, 2)
            kernel = mobility_tile(home_pos, col_pos, radius)
            return (accum + jnp.einsum('cdij,dvj->cvi', kernel, col_force, precision=lax.Precision.HIGHEST), None)
        starts = (jnp.arange(total // col_rows) * col_rows).astype(jnp.int32)
        init = jnp.zeros((3, forces.shape[1], home_rows), jnp.float32)
        result, _ = lax.scan(one_col, init, starts)
        return result
    home_starts = (jnp.arange(total // home_rows) * home_rows).astype(jnp.int32)
    blocks = lax.map(one_home, home_starts)
    return jnp.transpose(blocks, (1, 2, 0, 3)).reshape(3, forces.shape[1], total)
```

```python
import functools

import jax
import jax.numpy as jnp
from jax import lax
from jax.experimental import pallas as pl
from jax.experimental.pallas import tpu as pltpu
from jax.sharding import PartitionSpec as P

MESH = pl.DeviceIdType.MESH
F32 = jnp.float32
BF16 = jnp.bfloat16

radius_scale = 0.3

NX, NY, NZ = 4, 4, 16
PLANE = NX * NY * 2
REACH = NZ // 4
LANES = 128
ROWS = 32
HALF = ROWS // 2
GROUPS = LANES // HALF
FILL = 4


def place():
    blk, quad = lax.axis_index("blk"), lax.axis_index("quad")
    x = (quad // 2) * 2 + (blk // NZ) % 2
    return x, blk // (2 * NZ), blk % NZ, quad % 2


def device(x, y, z, core):
    return ((y * 2 + x % 2) * NZ + z, (x // 2) * 2 + core)


def plane_peers():
    offsets = [(a, b, c) for a in range(NX) for b in range(NY) for c in range(2)]
    far_first = sorted(offsets, key=lambda o: -(min(o[0], NX - o[0]) + min(o[1], NY - o[1])))
    return [o for o in far_first if o != (0, 0, 0)]


def target_offset(step):
    far = step - FILL
    rest = step - (FILL + NZ - 1 - 2 * REACH)
    sign = lambda odd: 1 - 2 * odd
    first = (REACH - step // 2) * sign(step % 2)
    middle = (NZ // 2 - (far + 1) // 2) * sign(1 - far % 2)
    last = (REACH - FILL // 2 - rest // 2) * sign(rest % 2)
    return jnp.where(step < FILL, first, jnp.where(far < NZ - 1 - 2 * REACH, middle, last))


def widened(value):
    return jnp.concatenate([value, jnp.zeros((value.shape[0], LANES - ROWS), F32)], axis=1)


def kernel(radius, pos_hbm, force_hbm, out_ref, pos_in, force_in, my_row, my_block, src_row, src_block, target_row,
           weights, src_pos, sent, landed, in_sem, send_sem, near_sem, far_sem, row_sem, block_sem, part_sem):
    x, y, z, core = place()
    plane_slot = x * GROUPS + y * 2 + core
    turn = (y * 2 + core) * HALF
    load_pos = pltpu.make_async_copy(pos_hbm, pos_in, in_sem.at[0])
    load_force = pltpu.make_async_copy(force_hbm, force_in, in_sem.at[1])
    load_pos.start()
    load_force.start()

    def in_plane(o):
        return device((x + o[0]) % NX, (y + o[1]) % NY, z, (core + o[2]) % 2)

    def on_line(k):
        return device(x, y, (z + k + NZ) % NZ, core)

    line = [k for d in range(REACH, 0, -1) for k in (d, -d)]
    barrier = pltpu.get_barrier_semaphore()
    for k in line:
        pl.semaphore_signal(barrier, 1, device_id=on_line(k), device_id_type=MESH)
    for o in plane_peers():
        pl.semaphore_signal(barrier, 1, device_id=in_plane(o), device_id_type=MESH)

    lane = lax.broadcasted_iota(jnp.int32, (8, LANES), 1)
    sub = lax.broadcasted_iota(jnp.int32, (8, LANES), 0)
    group = lane // HALF

    load_pos.wait()
    mine = [widened(pos_in[e : e + 1, :]) for e in range(3)]
    row = jnp.zeros((1, LANES), F32)
    for h in range(2):
        for e in range(3):
            m = 3 * h + e
            moved = pltpu.roll(mine[e], (HALF * (m - h)) % LANES, 1)
            row = jnp.where(group[0:1] == m, moved, row)
    my_row[0] = pltpu.roll(jnp.broadcast_to(row, (8, LANES)), turn, 1)[0:1]
    load_force.wait()
    parts = [widened(force_in[e]) for e in range(3)]
    dots = sum((mine[e] - 0.5) * parts[e] for e in range(3))
    stack = jnp.concatenate([*parts, dots], axis=0)
    stack = jnp.concatenate([stack, pltpu.roll(stack, LANES - HALF, 1)], axis=0)
    my_block[...] = jnp.transpose(stack)[0:HALF]

    pl.semaphore_wait(barrier, len(line) + len(plane_peers()))

    def send(src, dst, sem, where):
        pltpu.make_async_remote_copy(src, dst, send_sem, sem, device_id=where, device_id_type=MESH).start()

    for k in line:
        sem = near_sem.at[0 if k == -REACH else 1 if k == REACH else 2]
        send(my_row.at[0], target_row.at[z], sem, on_line(k))
    for o in plane_peers():
        send(my_row.at[0], src_row.at[plane_slot], row_sem, in_plane(o))
    for o in plane_peers():
        send(my_block, src_block.at[plane_slot], block_sem, in_plane(o))
    src_row[plane_slot] = my_row[0]
    src_block[plane_slot] = my_block[...]
    target_row[z] = my_row[0]

    def wait(ref, sem):
        pltpu.make_async_copy(ref, ref, sem).wait()

    up, down = (z + REACH) % NZ, (z + NZ - REACH) % NZ
    wait(my_row.at[0], near_sem.at[0])
    for k in range(REACH, 0, -1):
        send(target_row.at[up], target_row.at[up], far_sem, on_line(-k))
    wait(my_row.at[0], near_sem.at[1])
    for k in range(REACH - 1, 0, -1):
        send(target_row.at[down], target_row.at[down], far_sem, on_line(k))

    wait(src_row.at[pl.ds(0, PLANE - 1)], row_sem)
    for tile in range(PLANE // GROUPS):
        rows = jnp.concatenate([src_row[tile * GROUPS + k] for k in range(GROUPS)], axis=0)
        for h in range(2):
            for e in range(3):
                m = 3 * h + e
                own = jnp.sum(jnp.where((group - sub - m + 2 * GROUPS) % GROUPS == 0, rows, 0.0), axis=0, keepdims=True)
                at = (h * PLANE // GROUPS + tile) * LANES
                own = pltpu.roll(jnp.broadcast_to(own, (8, LANES)), (LANES - HALF * m) % LANES, 1)
                src_pos[e, :, at : at + LANES] = own
    wait(target_row.at[pl.ds(0, 2 * REACH - 2)], near_sem.at[2])

    wait(src_block.at[pl.ds(0, PLANE - 1)], block_sem)
    half_rows = PLANE * HALF
    value = src_block[...].reshape(half_rows, LANES)
    high = value.astype(BF16).astype(F32)
    low = value - high
    left = lax.broadcasted_iota(jnp.int32, (half_rows, LANES), 1) < LANES // 2
    weights[0:half_rows] = jnp.where(left, high, pltpu.roll(low, LANES // 2, 1)).astype(BF16)
    weights[half_rows:] = jnp.where(left, pltpu.roll(high, LANES // 2, 1), low).astype(BF16)

    wide = 2 * LANES
    near_sq = 4.0 * radius * radius
    lane_group = lax.broadcasted_iota(jnp.int32, (ROWS, LANES), 1) // HALF

    def one_target(step, carry):
        offset = target_offset(step)
        tz = (z + offset + NZ) % NZ

        @pl.when(step == FILL)
        def _():
            wait(target_row.at[pl.ds(0, NZ - 1 - 2 * REACH)], far_sem)

        theirs = pltpu.roll(jnp.broadcast_to(target_row[tz], (8, LANES)), LANES - turn, 1)
        columns = jnp.transpose(jnp.broadcast_to(theirs[0:1], (LANES, LANES)))
        home = [
            jnp.concatenate([columns[e * HALF : (e + 1) * HALF], columns[(3 + e) * HALF : (4 + e) * HALF]], axis=0)
            for e in range(3)
        ]
        total = jnp.zeros((4 * ROWS, LANES), F32)
        for p in range(2 * half_rows // wide):
            pieces = []
            for q in range(2):
                at = p * wide + q * LANES
                sep = [
                    (home[e].reshape(ROWS // 8, 8, LANES) - src_pos[e, :, at : at + LANES][None]).reshape(ROWS, LANES)
                    for e in range(3)
                ]
                squared = sep[0] * sep[0] + sep[1] * sep[1] + sep[2] * sep[2]
                inverse = lax.rsqrt(jnp.maximum(squared, 1e-30))
                inv_sq = inverse * inverse
                factor = (0.75 * radius) * inverse
                cubed = factor * inv_sq
                near = squared < near_sq
                iso = jnp.where(
                    near, 1.0 - (9.0 / 32.0 / radius) * (squared * inverse), factor + (2.0 / 3.0 * radius * radius) * cubed
                )
                dyad = jnp.where(
                    near,
                    (3.0 / 32.0 / radius) * jnp.minimum(inverse, 1000.0 / radius),
                    cubed * (1.0 - (2.0 * radius * radius) * inv_sq),
                )
                pieces.append(jnp.concatenate([dyad * s for s in sep] + [iso], axis=0))
            exact = jnp.concatenate(pieces, axis=1)
            upper = exact.astype(BF16)
            lower = (exact - upper.astype(F32)).astype(BF16)
            tile = weights[p * wide : (p + 1) * wide, :]
            total += jnp.dot(upper, tile, preferred_element_type=F32)
            total += jnp.dot(lower, tile, preferred_element_type=F32)

        which = lane_group % 4
        scale = jnp.where(which == 0, home[0] - 0.5, jnp.where(which == 1, home[1] - 0.5, jnp.where(which == 2, home[2] - 0.5, -1.0)))
        iso_part = total[3 * ROWS :]
        sums = []
        for c in range(3):
            both = scale * total[c * ROWS : (c + 1) * ROWS] + jnp.where(which == c, iso_part, 0.0)
            for shift in (64, 32, 16):
                both = both + pltpu.roll(both, shift, 1)
            sums += [both[8 * b : 8 * b + 8] for b in range(4)]
        first = sums[0]
        for g in range(1, 8):
            first = jnp.where(group == g, sums[g], first)
        second = sums[8]
        for g in range(1, 4):
            second = jnp.where(group % 4 == g, sums[8 + g], second)
        second = jnp.where(lane < 64, second, pltpu.roll(second, 4, 0))
        sent[step, 0:8] = first
        sent[step, 8:12] = second[0:4]

        @pl.when(offset != 0)
        def _():
            send(sent.at[step], landed.at[z], part_sem, device(x, y, tz, core))

        @pl.when(offset == 0)
        def _():
            landed[z] = sent[step]

        return carry

    lax.fori_loop(0, NZ, one_target, 0)

    wait(landed.at[pl.ds(0, NZ - 1)], part_sem)
    whole = landed[0]
    for k in range(1, NZ):
        whole = whole + landed[k]
    packed = jnp.concatenate([whole, jnp.zeros((LANES - 12, LANES), F32)], axis=0)
    turned = jnp.transpose(packed)
    out_lane = lax.broadcasted_iota(jnp.int32, (HALF, LANES), 1)
    for c in range(3):
        made = jnp.zeros((HALF, LANES), F32)
        for b in range(4):
            if c < 2:
                piece = turned[(c * 4 + b) * HALF : (c * 4 + b + 1) * HALF]
                made = jnp.where(out_lane // 8 == b, pltpu.roll(piece, 8 * b, 1) if b else piece, made)
            else:
                for u in range(2):
                    piece = turned[(u * 4 + b) * HALF : (u * 4 + b + 1) * HALF]
                    shift = (8 * b + 4 * u - 8) % LANES
                    made = jnp.where(out_lane // 4 == 2 * b + u, pltpu.roll(piece, shift, 1) if shift else piece, made)
        out_ref[c] = made[:, 0:ROWS]

    wait(target_row.at[pl.ds(0, 2 * REACH)], send_sem)
    wait(target_row.at[pl.ds(0, 2 * REACH - 1)], send_sem)
    wait(src_row.at[pl.ds(0, PLANE - 1)], send_sem)
    wait(src_block.at[pl.ds(0, PLANE - 1)], send_sem)
    wait(landed.at[pl.ds(0, NZ - 1)], send_sem)


def body(positions, forces):
    total = positions.shape[1] * lax.axis_size("blk") * lax.axis_size("quad")
    radius = radius_scale / total ** (1.0 / 3.0)
    dma = pltpu.SemaphoreType.DMA
    return pl.pallas_call(
        functools.partial(kernel, radius),
        out_shape=jax.ShapeDtypeStruct(forces.shape, F32),
        in_specs=[pl.BlockSpec(memory_space=pltpu.HBM)] * 2,
        out_specs=pl.BlockSpec(memory_space=pltpu.VMEM),
        scratch_shapes=[
            pltpu.VMEM((3, ROWS), F32),
            pltpu.VMEM((3, HALF, ROWS), F32),
            pltpu.VMEM((1, 1, LANES), F32),
            pltpu.VMEM((HALF, LANES), F32),
            pltpu.VMEM((PLANE, 1, LANES), F32),
            pltpu.VMEM((PLANE, HALF, LANES), F32),
            pltpu.VMEM((NZ, 1, LANES), F32),
            pltpu.VMEM((PLANE * ROWS, LANES), BF16),
            pltpu.VMEM((3, 8, PLANE * ROWS), F32),
            pltpu.VMEM((NZ, 12, LANES), F32),
            pltpu.VMEM((NZ, 12, LANES), F32),
            dma((2,)),
            dma,
            dma((3,)),
            dma,
            dma,
            dma,
            dma,
        ],
        compiler_params=pltpu.CompilerParams(collective_id=0, has_side_effects=True, vmem_limit_bytes=32 * 1024 * 1024),
    )(positions, forces)


def solution(mesh):
    in_specs = (P(None, ("blk", "quad")), P(None, None, ("blk", "quad")))
    out_specs = P(None, None, ("blk", "quad"))
    return jax.shard_map(body, mesh=mesh, in_specs=in_specs, out_specs=out_specs, check_vma=False)
```

```python
import functools

import jax
import jax.numpy as jnp
from jax import lax
from jax.experimental import pallas as pl
from jax.experimental.pallas import tpu as pltpu
from jax.sharding import PartitionSpec as P

MESH = pl.DeviceIdType.MESH
F32 = jnp.float32
BF16 = jnp.bfloat16

radius_scale = 0.3

NX, NY, NZ = 4, 4, 16
PLANE = NX * NY * 2
REACH = NZ // 4
LANES = 128
ROWS = 32
HALF = ROWS // 2
GROUPS = LANES // HALF


def place():
    blk, quad = lax.axis_index("blk"), lax.axis_index("quad")
    x = (quad // 2) * 2 + (blk // NZ) % 2
    return x, blk // (2 * NZ), blk % NZ, quad % 2


def device(x, y, z, core):
    return ((y * 2 + x % 2) * NZ + z, (x // 2) * 2 + core)


def plane_peers():
    offsets = [(a, b, c) for a in range(NX) for b in range(NY) for c in range(2)]
    far_first = sorted(offsets, key=lambda o: -(min(o[0], NX - o[0]) + min(o[1], NY - o[1])))
    return [o for o in far_first if o != (0, 0, 0)]


def widened(value):
    return jnp.concatenate([value, jnp.zeros((value.shape[0], LANES - ROWS), F32)], axis=1)


def kernel(radius, pos_hbm, force_hbm, out_ref, pos_in, force_in, my_row, my_block, src_row, src_block, target_row,
           weights, src_pos, sent, landed, in_sem, send_sem, line_sem, row_sem, block_sem, part_sem):
    x, y, z, core = place()
    plane_slot = x * GROUPS + y * 2 + core
    turn = (y * 2 + core) * HALF
    load_pos = pltpu.make_async_copy(pos_hbm, pos_in, in_sem.at[0])
    load_force = pltpu.make_async_copy(force_hbm, force_in, in_sem.at[1])
    load_pos.start()
    load_force.start()

    def in_plane(o):
        return device((x + o[0]) % NX, (y + o[1]) % NY, z, (core + o[2]) % 2)

    def on_line(k):
        return device(x, y, (z + k + NZ) % NZ, core)

    line = [k for d in range(REACH, 0, -1) for k in (d, -d)]
    barrier = pltpu.get_barrier_semaphore()
    for k in line:
        pl.semaphore_signal(barrier, 1, device_id=on_line(k), device_id_type=MESH)
    for o in plane_peers():
        pl.semaphore_signal(barrier, 1, device_id=in_plane(o), device_id_type=MESH)

    lane = lax.broadcasted_iota(jnp.int32, (8, LANES), 1)
    sub = lax.broadcasted_iota(jnp.int32, (8, LANES), 0)
    group = lane // HALF

    load_pos.wait()
    mine = [widened(pos_in[e : e + 1, :]) for e in range(3)]
    row = jnp.zeros((1, LANES), F32)
    for h in range(2):
        for e in range(3):
            m = 3 * h + e
            moved = pltpu.roll(mine[e], (HALF * (m - h)) % LANES, 1)
            row = jnp.where(group[0:1] == m, moved, row)
    my_row[0] = pltpu.roll(jnp.broadcast_to(row, (8, LANES)), turn, 1)[0:1]
    load_force.wait()
    parts = [widened(force_in[e]) for e in range(3)]
    dots = sum((mine[e] - 0.5) * parts[e] for e in range(3))
    stack = jnp.concatenate([*parts, dots], axis=0)
    stack = jnp.concatenate([stack, pltpu.roll(stack, LANES - HALF, 1)], axis=0)
    my_block[...] = jnp.transpose(stack)[0:HALF]

    pl.semaphore_wait(barrier, len(line) + len(plane_peers()))

    def send(src, dst, sem, where):
        pltpu.make_async_remote_copy(src, dst, send_sem, sem, device_id=where, device_id_type=MESH).start()

    for k in line:
        send(my_row.at[0], target_row.at[z], line_sem.at[z], on_line(k))
    for o in plane_peers():
        send(my_row.at[0], src_row.at[plane_slot], row_sem, in_plane(o))
    for o in plane_peers():
        send(my_block, src_block.at[plane_slot], block_sem, in_plane(o))
    src_row[plane_slot] = my_row[0]
    src_block[plane_slot] = my_block[...]
    target_row[z] = my_row[0]

    def wait(ref, sem):
        pltpu.make_async_copy(ref, ref, sem).wait()

    up, down = (z + REACH) % NZ, (z + NZ - REACH) % NZ
    wait(target_row.at[up], line_sem.at[up])
    for k in range(REACH, 0, -1):
        send(target_row.at[up], target_row.at[up], line_sem.at[up], on_line(-k))
    wait(target_row.at[down], line_sem.at[down])
    for k in range(REACH - 1, 0, -1):
        send(target_row.at[down], target_row.at[down], line_sem.at[down], on_line(k))

    wait(src_row.at[pl.ds(0, PLANE - 1)], row_sem)
    for tile in range(PLANE // GROUPS):
        rows = jnp.concatenate([src_row[tile * GROUPS + k] for k in range(GROUPS)], axis=0)
        for h in range(2):
            for e in range(3):
                m = 3 * h + e
                own = jnp.sum(jnp.where((group - sub - m + 2 * GROUPS) % GROUPS == 0, rows, 0.0), axis=0, keepdims=True)
                at = (h * PLANE // GROUPS + tile) * LANES
                own = pltpu.roll(jnp.broadcast_to(own, (8, LANES)), (LANES - HALF * m) % LANES, 1)
                src_pos[e, :, at : at + LANES] = own

    wait(src_block.at[pl.ds(0, PLANE - 1)], block_sem)
    half_rows = PLANE * HALF
    value = src_block[...].reshape(half_rows, LANES)
    high = value.astype(BF16).astype(F32)
    low = value - high
    left = lax.broadcasted_iota(jnp.int32, (half_rows, LANES), 1) < LANES // 2
    weights[0:half_rows] = jnp.where(left, high, pltpu.roll(low, LANES // 2, 1)).astype(BF16)
    weights[half_rows:] = jnp.where(left, pltpu.roll(high, LANES // 2, 1), low).astype(BF16)

    wide = 2 * LANES
    near_sq = 4.0 * radius * radius
    lane_group = lax.broadcasted_iota(jnp.int32, (ROWS, LANES), 1) // HALF

    which = lane_group % 4

    def arrived(tz):
        @pl.when((tz < NZ) & (tz != z) & (tz != up) & (tz != down))
        def _():
            wait(target_row.at[tz], line_sem.at[tz])

    def columns(tz):
        theirs = pltpu.roll(jnp.broadcast_to(target_row[tz], (8, LANES)), LANES - turn, 1)
        turned = jnp.transpose(jnp.broadcast_to(theirs[0:1], (LANES, LANES)))
        return [
            jnp.concatenate([turned[e * HALF : (e + 1) * HALF], turned[(3 + e) * HALF : (4 + e) * HALF]], axis=0)
            for e in range(3)
        ]

    def pair_sums(home):
        total = jnp.zeros((4 * ROWS, LANES), F32)
        for p in range(2 * half_rows // wide):
            pieces = []
            for q in range(2):
                at = p * wide + q * LANES
                sep = [
                    (home[e].reshape(ROWS // 8, 8, LANES) - src_pos[e, :, at : at + LANES][None]).reshape(ROWS, LANES)
                    for e in range(3)
                ]
                squared = sep[0] * sep[0] + sep[1] * sep[1] + sep[2] * sep[2]
                inverse = lax.rsqrt(jnp.maximum(squared, 1e-30))
                inv_sq = inverse * inverse
                factor = (0.75 * radius) * inverse
                cubed = factor * inv_sq
                near = squared < near_sq
                iso = jnp.where(
                    near, 1.0 - (9.0 / 32.0 / radius) * (squared * inverse), factor + (2.0 / 3.0 * radius * radius) * cubed
                )
                dyad = jnp.where(
                    near,
                    (3.0 / 32.0 / radius) * jnp.minimum(inverse, 1000.0 / radius),
                    cubed * (1.0 - (2.0 * radius * radius) * inv_sq),
                )
                pieces.append(jnp.concatenate([dyad * s for s in sep] + [iso], axis=0))
            exact = jnp.concatenate(pieces, axis=1)
            upper = exact.astype(BF16)
            lower = (exact - upper.astype(F32)).astype(BF16)
            tile = weights[p * wide : (p + 1) * wide, :]
            total += jnp.dot(upper, tile, preferred_element_type=F32)
            total += jnp.dot(lower, tile, preferred_element_type=F32)
        scale = jnp.where(
            which == 0, home[0] - 0.5, jnp.where(which == 1, home[1] - 0.5, jnp.where(which == 2, home[2] - 0.5, -1.0))
        )
        iso_part = total[3 * ROWS :]
        return [
            scale * total[c * ROWS : (c + 1) * ROWS] + jnp.where(which == c, iso_part, 0.0) for c in range(3)
        ]

    def fold(spread, tz):
        sums = []
        for both in spread:
            for shift in (64, 32, 16):
                both = both + pltpu.roll(both, shift, 1)
            sums += [both[8 * b : 8 * b + 8] for b in range(4)]
        first = sums[0]
        for g in range(1, 8):
            first = jnp.where(group == g, sums[g], first)
        second = sums[8]
        for g in range(1, 4):
            second = jnp.where(group % 4 == g, sums[8 + g], second)
        second = jnp.where(lane < 64, second, pltpu.roll(second, 4, 0))
        sent[tz, 0:8] = first
        sent[tz, 8:12] = second[0:4]

    def give(tz):
        @pl.when((tz >= 0) & (tz != z))
        def _():
            send(sent.at[tz], landed.at[z], part_sem, device(x, y, tz, core))

        @pl.when(tz == z)
        def _():
            landed[z] = sent[z]

    def one_target(tz, carry):
        home, spread = carry
        arrived(tz + 1)
        later = columns(jnp.minimum(tz + 1, NZ - 1))
        fold(spread, jnp.maximum(tz - 1, 0))
        spread = pair_sums(home)
        give(tz - 1)
        return later, spread

    arrived(0)
    zeros = [jnp.zeros((ROWS, LANES), F32)] * 3
    _, spread = lax.fori_loop(0, NZ, one_target, (columns(0), zeros))
    fold(spread, NZ - 1)
    give(jnp.int32(NZ - 1))

    wait(landed.at[pl.ds(0, NZ - 1)], part_sem)
    whole = landed[0]
    for k in range(1, NZ):
        whole = whole + landed[k]
    packed = jnp.concatenate([whole, jnp.zeros((LANES - 12, LANES), F32)], axis=0)
    turned = jnp.transpose(packed)
    out_lane = lax.broadcasted_iota(jnp.int32, (HALF, LANES), 1)
    for c in range(3):
        made = jnp.zeros((HALF, LANES), F32)
        for b in range(4):
            if c < 2:
                piece = turned[(c * 4 + b) * HALF : (c * 4 + b + 1) * HALF]
                made = jnp.where(out_lane // 8 == b, pltpu.roll(piece, 8 * b, 1) if b else piece, made)
            else:
                for u in range(2):
                    piece = turned[(u * 4 + b) * HALF : (u * 4 + b + 1) * HALF]
                    shift = (8 * b + 4 * u - 8) % LANES
                    made = jnp.where(out_lane // 4 == 2 * b + u, pltpu.roll(piece, shift, 1) if shift else piece, made)
        out_ref[c] = made[:, 0:ROWS]

    wait(target_row.at[pl.ds(0, 2 * REACH)], send_sem)
    wait(target_row.at[pl.ds(0, 2 * REACH - 1)], send_sem)
    wait(src_row.at[pl.ds(0, PLANE - 1)], send_sem)
    wait(src_block.at[pl.ds(0, PLANE - 1)], send_sem)
    wait(landed.at[pl.ds(0, NZ - 1)], send_sem)


def body(positions, forces):
    total = positions.shape[1] * lax.axis_size("blk") * lax.axis_size("quad")
    radius = radius_scale / total ** (1.0 / 3.0)
    dma = pltpu.SemaphoreType.DMA
    return pl.pallas_call(
        functools.partial(kernel, radius),
        out_shape=jax.ShapeDtypeStruct(forces.shape, F32),
        in_specs=[pl.BlockSpec(memory_space=pltpu.HBM)] * 2,
        out_specs=pl.BlockSpec(memory_space=pltpu.VMEM),
        scratch_shapes=[
            pltpu.VMEM((3, ROWS), F32),
            pltpu.VMEM((3, HALF, ROWS), F32),
            pltpu.VMEM((1, 1, LANES), F32),
            pltpu.VMEM((HALF, LANES), F32),
            pltpu.VMEM((PLANE, 1, LANES), F32),
            pltpu.VMEM((PLANE, HALF, LANES), F32),
            pltpu.VMEM((NZ, 1, LANES), F32),
            pltpu.VMEM((PLANE * ROWS, LANES), BF16),
            pltpu.VMEM((3, 8, PLANE * ROWS), F32),
            pltpu.VMEM((NZ, 12, LANES), F32),
            pltpu.VMEM((NZ, 12, LANES), F32),
            dma((2,)),
            dma,
            dma((NZ,)),
            dma,
            dma,
            dma,
        ],
        compiler_params=pltpu.CompilerParams(collective_id=0, has_side_effects=True, vmem_limit_bytes=32 * 1024 * 1024),
    )(*(pltpu.with_memory_space_constraint(a, pltpu.HBM) for a in (positions, forces)))


def solution(mesh):
    in_specs = (P(None, ("blk", "quad")), P(None, None, ("blk", "quad")))
    out_specs = P(None, None, ("blk", "quad"))
    return jax.shard_map(body, mesh=mesh, in_specs=in_specs, out_specs=out_specs, check_vma=False)
```

```python
import functools

import jax
import jax.numpy as jnp
from jax import lax
from jax.experimental import pallas as pl
from jax.experimental.pallas import tpu as pltpu
from jax.sharding import PartitionSpec as P

MESH = pl.DeviceIdType.MESH
F32 = jnp.float32
BF16 = jnp.bfloat16

radius_scale = 0.3

NX, NY, NZ = 4, 4, 16
CHIPS = NX * NY
PLANE = CHIPS * 2
REACH = NZ // 4
LANES = 128
ROWS = 32
HALF = ROWS // 2
GROUPS = LANES // HALF
SOON = 12


def place():
    blk, quad = lax.axis_index("blk"), lax.axis_index("quad")
    x = (quad // 2) * 2 + (blk // NZ) % 2
    return x, blk // (2 * NZ), blk % NZ, quad % 2


def device(x, y, z, core):
    return ((y * 2 + x % 2) * NZ + z, (x // 2) * 2 + core)


def slot_of(x, y):
    return (x // 2) * 8 + (y // 2) * 4 + (x % 2) * 2 + y % 2


def slot_device(slot, z, core):
    return device((slot // 8) * 2 + (slot // 2) % 2, ((slot // 4) % 2) * 2 + slot % 2, z, core)


def widened(value):
    return jnp.concatenate([value, jnp.zeros((value.shape[0], LANES - ROWS), F32)], axis=1)


def kernel(radius, pos_hbm, force_hbm, out_ref, pos_in, force_in, my_row, my_block, src_row, src_block, target_row,
           weights, src_pos, sent, landed, in_sem, send_sem, line_sem, row_sem, block_sem, part_sem, open_sem):
    x, y, z, core = place()
    plane_slot = slot_of(x, y)
    sibling = device(x, y, z, 1 - core)
    turn = (plane_slot % GROUPS) * HALF
    load_pos = pltpu.make_async_copy(pos_hbm, pos_in, in_sem.at[0])
    load_force = pltpu.make_async_copy(force_hbm, force_in, in_sem.at[1])
    load_pos.start()
    load_force.start()

    def on_line(k):
        return device(x, y, (z + k + NZ) % NZ, core)

    line = [k for d in range(REACH, 0, -1) for k in (d, -d)]
    barrier = pltpu.get_barrier_semaphore()
    for k in line:
        pl.semaphore_signal(barrier, 1, device_id=on_line(k), device_id_type=MESH)
    @pl.loop(0, CHIPS - 1 - plane_slot)
    def _(k):
        pl.semaphore_signal(barrier, 1, device_id=slot_device(CHIPS - 1 - k, z, core), device_id_type=MESH)

    pl.semaphore_signal(barrier, 1, device_id=sibling, device_id_type=MESH)

    lane = lax.broadcasted_iota(jnp.int32, (8, LANES), 1)
    sub = lax.broadcasted_iota(jnp.int32, (8, LANES), 0)
    group = lane // HALF

    load_pos.wait()
    mine = [widened(pos_in[e : e + 1, :]) for e in range(3)]
    row = jnp.zeros((1, LANES), F32)
    for h in range(2):
        for e in range(3):
            m = 3 * h + e
            moved = pltpu.roll(mine[e], (HALF * (m - h)) % LANES, 1)
            row = jnp.where(group[0:1] == m, moved, row)
    my_row[0] = pltpu.roll(jnp.broadcast_to(row, (8, LANES)), turn, 1)[0:1]
    load_force.wait()
    parts = [widened(force_in[e]) for e in range(3)]
    dots = sum((mine[e] - 0.5) * parts[e] for e in range(3))
    stack = jnp.concatenate([*parts, dots], axis=0)
    stack = jnp.concatenate([stack, pltpu.roll(stack, LANES - HALF, 1)], axis=0)
    my_block[...] = jnp.transpose(stack)[0:HALF]

    pl.semaphore_wait(barrier, len(line) + 1 + plane_slot)

    def send(src, dst, sem, where):
        pltpu.make_async_remote_copy(src, dst, send_sem, sem, device_id=where, device_id_type=MESH).start()

    for k in line:
        send(my_row.at[0], target_row.at[z], line_sem.at[z], on_line(k))
    def send_sources(slot):
        send(my_row.at[0], src_row.at[0, plane_slot], row_sem.at[0], slot_device(slot, z, core))
        send(my_block, src_block.at[0, plane_slot], block_sem.at[0], slot_device(slot, z, core))

    @pl.loop(0, plane_slot)
    def _(slot):
        pl.semaphore_signal(open_sem.at[plane_slot], 1, device_id=slot_device(slot, z, core), device_id_type=MESH)
        send_sources(slot)

    src_row[0, plane_slot] = my_row[0]
    src_block[0, plane_slot] = my_block[...]
    target_row[z] = my_row[0]

    def wait(ref, sem):
        pltpu.make_async_copy(ref, ref, sem).wait()

    def open_to(first, last):
        @pl.loop(first, last)
        def _(slot):
            pl.semaphore_wait(open_sem.at[slot], 1)
            send_sources(slot)

    open_to(plane_slot + 1, jnp.maximum(plane_slot + 1, SOON))

    up, down = (z + REACH) % NZ, (z + NZ - REACH) % NZ
    wait(target_row.at[up], line_sem.at[up])
    for k in range(REACH, 0, -1):
        send(target_row.at[up], target_row.at[up], line_sem.at[up], on_line(-k))
    wait(target_row.at[down], line_sem.at[down])
    for k in range(REACH - 1, 0, -1):
        send(target_row.at[down], target_row.at[down], line_sem.at[down], on_line(k))

    open_to(jnp.maximum(plane_slot + 1, SOON), CHIPS)

    half_rows = PLANE * HALF
    core_rows = CHIPS * HALF
    left = lax.broadcasted_iota(jnp.int32, (core_rows, LANES), 1) < LANES // 2

    def prepare(i):
        for tile in range(CHIPS // GROUPS):
            rows = jnp.concatenate([src_row[i, tile * GROUPS + k] for k in range(GROUPS)], axis=0)
            for h in range(2):
                for e in range(3):
                    m = 3 * h + e
                    own = jnp.sum(
                        jnp.where((group - sub - m + 2 * GROUPS) % GROUPS == 0, rows, 0.0), axis=0, keepdims=True
                    )
                    at = (h * (PLANE // GROUPS) + i * (CHIPS // GROUPS) + tile) * LANES
                    own = pltpu.roll(jnp.broadcast_to(own, (8, LANES)), (LANES - HALF * m) % LANES, 1)
                    src_pos[e, :, at : at + LANES] = own
        value = src_block[i].reshape(core_rows, LANES)
        high = value.astype(BF16).astype(F32)
        low = value - high
        at = i * core_rows
        weights[at : at + core_rows] = jnp.where(left, high, pltpu.roll(low, LANES // 2, 1)).astype(BF16)
        at = at + half_rows
        weights[at : at + core_rows] = jnp.where(left, pltpu.roll(high, LANES // 2, 1), low).astype(BF16)

    wait(src_row.at[0, pl.ds(0, CHIPS - 1)], row_sem.at[0])
    send(src_row.at[0], src_row.at[1], row_sem.at[1], sibling)
    wait(src_block.at[0, pl.ds(0, CHIPS - 1)], block_sem.at[0])
    send(src_block.at[0], src_block.at[1], block_sem.at[1], sibling)
    prepare(0)
    wait(src_row.at[1], row_sem.at[1])
    wait(src_block.at[1], block_sem.at[1])
    prepare(1)

    wide = 2 * LANES
    near_sq = 4.0 * radius * radius
    lane_group = lax.broadcasted_iota(jnp.int32, (ROWS, LANES), 1) // HALF

    which = lane_group % 4

    def arrived(tz):
        @pl.when((tz < NZ) & (tz != z) & (tz != up) & (tz != down))
        def _():
            wait(target_row.at[tz], line_sem.at[tz])

    def columns(tz):
        theirs = pltpu.roll(jnp.broadcast_to(target_row[tz], (8, LANES)), LANES - turn, 1)
        turned = jnp.transpose(jnp.broadcast_to(theirs[0:1], (LANES, LANES)))
        return [
            jnp.concatenate([turned[e * HALF : (e + 1) * HALF], turned[(3 + e) * HALF : (4 + e) * HALF]], axis=0)
            for e in range(3)
        ]

    def pair_sums(home):
        total = jnp.zeros((4 * ROWS, LANES), F32)
        for p in range(2 * half_rows // wide):
            pieces = []
            for q in range(2):
                at = p * wide + q * LANES
                sep = [
                    (home[e].reshape(ROWS // 8, 8, LANES) - src_pos[e, :, at : at + LANES][None]).reshape(ROWS, LANES)
                    for e in range(3)
                ]
                squared = sep[0] * sep[0] + sep[1] * sep[1] + sep[2] * sep[2]
                inverse = lax.rsqrt(jnp.maximum(squared, 1e-30))
                inv_sq = inverse * inverse
                factor = (0.75 * radius) * inverse
                cubed = factor * inv_sq
                near = squared < near_sq
                iso = jnp.where(
                    near, 1.0 - (9.0 / 32.0 / radius) * (squared * inverse), factor + (2.0 / 3.0 * radius * radius) * cubed
                )
                dyad = jnp.where(
                    near,
                    (3.0 / 32.0 / radius) * jnp.minimum(inverse, 1000.0 / radius),
                    cubed * (1.0 - (2.0 * radius * radius) * inv_sq),
                )
                pieces.append(jnp.concatenate([dyad * s for s in sep] + [iso], axis=0))
            exact = jnp.concatenate(pieces, axis=1)
            upper = exact.astype(BF16)
            lower = (exact - upper.astype(F32)).astype(BF16)
            tile = weights[p * wide : (p + 1) * wide, :]
            total += jnp.dot(
                jnp.concatenate([upper, lower], axis=1), jnp.concatenate([tile, tile], axis=0), preferred_element_type=F32
            )
        scale = jnp.where(
            which == 0, home[0] - 0.5, jnp.where(which == 1, home[1] - 0.5, jnp.where(which == 2, home[2] - 0.5, -1.0))
        )
        iso_part = total[3 * ROWS :]
        return [
            scale * total[c * ROWS : (c + 1) * ROWS] + jnp.where(which == c, iso_part, 0.0) for c in range(3)
        ]

    def fold(spread, tz):
        sums = []
        for both in spread:
            for shift in (64, 32, 16):
                both = both + pltpu.roll(both, shift, 1)
            sums += [both[8 * b : 8 * b + 8] for b in range(4)]
        first = sums[0]
        for g in range(1, 8):
            first = jnp.where(group == g, sums[g], first)
        second = sums[8]
        for g in range(1, 4):
            second = jnp.where(group % 4 == g, sums[8 + g], second)
        second = jnp.where(lane < 64, second, pltpu.roll(second, 4, 0))
        sent[tz, 0:8] = first
        sent[tz, 8:12] = second[0:4]

    def give(tz):
        @pl.when((tz >= 0) & (tz != z))
        def _():
            send(sent.at[tz], landed.at[z], part_sem, device(x, y, tz, core))

        @pl.when(tz == z)
        def _():
            landed[z] = sent[z]

    def one_target(tz, carry):
        home, spread = carry
        arrived(tz + 1)
        later = columns(jnp.minimum(tz + 1, NZ - 1))
        fold(spread, jnp.maximum(tz - 1, 0))
        spread = pair_sums(home)
        give(tz - 1)
        return later, spread

    arrived(0)
    zeros = [jnp.zeros((ROWS, LANES), F32)] * 3
    _, spread = lax.fori_loop(0, NZ, one_target, (columns(0), zeros))
    fold(spread, NZ - 1)
    give(jnp.int32(NZ - 1))

    wait(landed.at[pl.ds(0, NZ - 1)], part_sem)
    whole = landed[0]
    for k in range(1, NZ):
        whole = whole + landed[k]
    packed = jnp.concatenate([whole, jnp.zeros((LANES - 12, LANES), F32)], axis=0)
    turned = jnp.transpose(packed)
    out_lane = lax.broadcasted_iota(jnp.int32, (HALF, LANES), 1)
    for c in range(3):
        made = jnp.zeros((HALF, LANES), F32)
        for b in range(4):
            if c < 2:
                piece = turned[(c * 4 + b) * HALF : (c * 4 + b + 1) * HALF]
                made = jnp.where(out_lane // 8 == b, pltpu.roll(piece, 8 * b, 1) if b else piece, made)
            else:
                for u in range(2):
                    piece = turned[(u * 4 + b) * HALF : (u * 4 + b + 1) * HALF]
                    shift = (8 * b + 4 * u - 8) % LANES
                    made = jnp.where(out_lane // 4 == 2 * b + u, pltpu.roll(piece, shift, 1) if shift else piece, made)
        out_ref[c] = made[:, 0:ROWS]

    wait(target_row.at[pl.ds(0, 2 * REACH)], send_sem)
    wait(target_row.at[pl.ds(0, 2 * REACH - 1)], send_sem)
    wait(src_row.at[0, pl.ds(0, CHIPS - 1)], send_sem)
    wait(src_row.at[1], send_sem)
    wait(src_block.at[0, pl.ds(0, CHIPS - 1)], send_sem)
    wait(src_block.at[1], send_sem)
    wait(landed.at[pl.ds(0, NZ - 1)], send_sem)


def body(positions, forces):
    total = positions.shape[1] * lax.axis_size("blk") * lax.axis_size("quad")
    radius = radius_scale / total ** (1.0 / 3.0)
    dma = pltpu.SemaphoreType.DMA
    return pl.pallas_call(
        functools.partial(kernel, radius),
        out_shape=jax.ShapeDtypeStruct(forces.shape, F32),
        in_specs=[pl.BlockSpec(memory_space=pltpu.HBM)] * 2,
        out_specs=pl.BlockSpec(memory_space=pltpu.VMEM),
        scratch_shapes=[
            pltpu.VMEM((3, ROWS), F32),
            pltpu.VMEM((3, HALF, ROWS), F32),
            pltpu.VMEM((1, 1, LANES), F32),
            pltpu.VMEM((HALF, LANES), F32),
            pltpu.VMEM((2, CHIPS, 1, LANES), F32),
            pltpu.VMEM((2, CHIPS, HALF, LANES), F32),
            pltpu.VMEM((NZ, 1, LANES), F32),
            pltpu.VMEM((PLANE * ROWS, LANES), BF16),
            pltpu.VMEM((3, 8, PLANE * ROWS), F32),
            pltpu.VMEM((NZ, 12, LANES), F32),
            pltpu.VMEM((NZ, 12, LANES), F32),
            dma((2,)),
            dma,
            dma((NZ,)),
            dma((2,)),
            dma((2,)),
            dma,
            pltpu.SemaphoreType.REGULAR((CHIPS,)),
        ],
        compiler_params=pltpu.CompilerParams(collective_id=0, has_side_effects=True, vmem_limit_bytes=32 * 1024 * 1024),
    )(*(pltpu.with_memory_space_constraint(a, pltpu.HBM) for a in (positions, forces)))


def solution(mesh):
    in_specs = (P(None, ("blk", "quad")), P(None, None, ("blk", "quad")))
    out_specs = P(None, None, ("blk", "quad"))
    return jax.shard_map(body, mesh=mesh, in_specs=in_specs, out_specs=out_specs, check_vma=False)
```

```python
import functools

import jax
import jax.numpy as jnp
from jax import lax
from jax.experimental import pallas as pl
from jax.experimental.pallas import tpu as pltpu
from jax.sharding import PartitionSpec as P

MESH = pl.DeviceIdType.MESH
F32 = jnp.float32
BF16 = jnp.bfloat16

radius_scale = 0.3

NX, NY, NZ = 4, 4, 16
CHIPS = NX * NY
PLANE = CHIPS * 2
REACH = NZ // 4
LANES = 128
ROWS = 32
HALF = ROWS // 2
GROUPS = LANES // HALF
SOON = 12


def place():
    blk, quad = lax.axis_index("blk"), lax.axis_index("quad")
    x = (quad // 2) * 2 + (blk // NZ) % 2
    return x, blk // (2 * NZ), blk % NZ, quad % 2


def device(x, y, z, core):
    return ((y * 2 + x % 2) * NZ + z, (x // 2) * 2 + core)


def slot_of(x, y):
    return (x // 2) * 8 + (y // 2) * 4 + (x % 2) * 2 + y % 2


def slot_device(slot, z, core):
    return device((slot // 8) * 2 + (slot // 2) % 2, ((slot // 4) % 2) * 2 + slot % 2, z, core)


def widened(value):
    return jnp.concatenate([value, jnp.zeros((value.shape[0], LANES - ROWS), F32)], axis=1)


def kernel(radius, pos_hbm, force_hbm, out_ref, pos_in, force_in, my_row, my_block, src_row, src_block, target_row,
           weights, src_pos, sent, landed, in_sem, send_sem, line_sem, row_sem, block_sem, part_sem, open_sem):
    x, y, z, core = place()
    plane_slot = slot_of(x, y)
    sibling = device(x, y, z, 1 - core)
    early = plane_slot < SOON
    met = jnp.where(early, SOON, CHIPS)
    turn = (plane_slot % GROUPS) * HALF
    load_pos = pltpu.make_async_copy(pos_hbm, pos_in, in_sem.at[0])
    load_force = pltpu.make_async_copy(force_hbm, force_in, in_sem.at[1])
    load_pos.start()
    load_force.start()

    def on_line(k):
        return device(x, y, (z + k + NZ) % NZ, core)

    line = [k for d in range(REACH, 0, -1) for k in (d, -d)]
    barrier = pltpu.get_barrier_semaphore()
    for k in line:
        pl.semaphore_signal(barrier, 1, device_id=on_line(k), device_id_type=MESH)
    @pl.loop(jnp.where(early, 0, SOON), CHIPS)
    def _(slot):
        @pl.when(slot != plane_slot)
        def _():
            pl.semaphore_signal(barrier, 1, device_id=slot_device(slot, z, core), device_id_type=MESH)

    pl.semaphore_signal(barrier, 1, device_id=sibling, device_id_type=MESH)

    lane = lax.broadcasted_iota(jnp.int32, (8, LANES), 1)
    sub = lax.broadcasted_iota(jnp.int32, (8, LANES), 0)
    group = lane // HALF

    load_pos.wait()
    mine = [widened(pos_in[e : e + 1, :]) for e in range(3)]
    row = jnp.zeros((1, LANES), F32)
    for h in range(2):
        for e in range(3):
            m = 3 * h + e
            moved = pltpu.roll(mine[e], (HALF * (m - h)) % LANES, 1)
            row = jnp.where(group[0:1] == m, moved, row)
    my_row[0] = pltpu.roll(jnp.broadcast_to(row, (8, LANES)), turn, 1)[0:1]
    load_force.wait()
    parts = [widened(force_in[e]) for e in range(3)]
    dots = sum((mine[e] - 0.5) * parts[e] for e in range(3))
    stack = jnp.concatenate([*parts, dots], axis=0)
    stack = jnp.concatenate([stack, pltpu.roll(stack, LANES - HALF, 1)], axis=0)
    my_block[...] = jnp.transpose(stack)[0:HALF]

    pl.semaphore_wait(barrier, len(line) + met)

    def send(src, dst, sem, where):
        pltpu.make_async_remote_copy(src, dst, send_sem, sem, device_id=where, device_id_type=MESH).start()

    for k in line:
        send(my_row.at[0], target_row.at[z], line_sem.at[z], on_line(k))
    def send_sources(slot):
        send(my_row.at[0], src_row.at[0, plane_slot], row_sem.at[0], slot_device(slot, z, core))
        send(my_block, src_block.at[0, plane_slot], block_sem.at[0], slot_device(slot, z, core))

    @pl.loop(0, met)
    def _(slot):
        @pl.when(jnp.logical_not(early) & (slot < SOON))
        def _():
            pl.semaphore_signal(open_sem.at[plane_slot], 1, device_id=slot_device(slot, z, core), device_id_type=MESH)

        @pl.when(slot != plane_slot)
        def _():
            send_sources(slot)

    src_row[0, plane_slot] = my_row[0]
    src_block[0, plane_slot] = my_block[...]
    target_row[z] = my_row[0]

    def wait(ref, sem):
        pltpu.make_async_copy(ref, ref, sem).wait()

    up, down = (z + REACH) % NZ, (z + NZ - REACH) % NZ
    wait(target_row.at[up], line_sem.at[up])
    for k in range(REACH, 0, -1):
        send(target_row.at[up], target_row.at[up], line_sem.at[up], on_line(-k))
    wait(target_row.at[down], line_sem.at[down])
    for k in range(REACH - 1, 0, -1):
        send(target_row.at[down], target_row.at[down], line_sem.at[down], on_line(k))

    @pl.loop(met, CHIPS)
    def _(slot):
        pl.semaphore_wait(open_sem.at[slot], 1)
        send_sources(slot)

    half_rows = PLANE * HALF
    core_rows = CHIPS * HALF
    left = lax.broadcasted_iota(jnp.int32, (core_rows, LANES), 1) < LANES // 2

    def prepare(i):
        for tile in range(CHIPS // GROUPS):
            rows = jnp.concatenate([src_row[i, tile * GROUPS + k] for k in range(GROUPS)], axis=0)
            for h in range(2):
                for e in range(3):
                    m = 3 * h + e
                    own = jnp.sum(
                        jnp.where((group - sub - m + 2 * GROUPS) % GROUPS == 0, rows, 0.0), axis=0, keepdims=True
                    )
                    at = (h * (PLANE // GROUPS) + i * (CHIPS // GROUPS) + tile) * LANES
                    own = pltpu.roll(jnp.broadcast_to(own, (8, LANES)), (LANES - HALF * m) % LANES, 1)
                    src_pos[e, :, at : at + LANES] = own
        value = src_block[i].reshape(core_rows, LANES)
        high = value.astype(BF16).astype(F32)
        low = value - high
        at = i * core_rows
        weights[at : at + core_rows] = jnp.where(left, high, pltpu.roll(low, LANES // 2, 1)).astype(BF16)
        at = at + half_rows
        weights[at : at + core_rows] = jnp.where(left, pltpu.roll(high, LANES // 2, 1), low).astype(BF16)

    wait(src_row.at[0, pl.ds(0, CHIPS - 1)], row_sem.at[0])
    send(src_row.at[0], src_row.at[1], row_sem.at[1], sibling)
    wait(src_block.at[0, pl.ds(0, CHIPS - 1)], block_sem.at[0])
    send(src_block.at[0], src_block.at[1], block_sem.at[1], sibling)
    prepare(0)
    wait(src_row.at[1], row_sem.at[1])
    wait(src_block.at[1], block_sem.at[1])
    prepare(1)

    wide = 2 * LANES
    near_sq = 4.0 * radius * radius
    lane_group = lax.broadcasted_iota(jnp.int32, (ROWS, LANES), 1) // HALF

    which = lane_group % 4

    def arrived(tz):
        @pl.when((tz < NZ) & (tz != z) & (tz != up) & (tz != down))
        def _():
            wait(target_row.at[tz], line_sem.at[tz])

    def columns(tz):
        theirs = pltpu.roll(jnp.broadcast_to(target_row[tz], (8, LANES)), LANES - turn, 1)
        turned = jnp.transpose(jnp.broadcast_to(theirs[0:1], (LANES, LANES)))
        return [
            jnp.concatenate([turned[e * HALF : (e + 1) * HALF], turned[(3 + e) * HALF : (4 + e) * HALF]], axis=0)
            for e in range(3)
        ]

    def pair_sums(home):
        total = jnp.zeros((4 * ROWS, LANES), F32)
        for p in range(2 * half_rows // wide):
            pieces = []
            for q in range(2):
                at = p * wide + q * LANES
                sep = [
                    (home[e].reshape(ROWS // 8, 8, LANES) - src_pos[e, :, at : at + LANES][None]).reshape(ROWS, LANES)
                    for e in range(3)
                ]
                squared = sep[0] * sep[0] + sep[1] * sep[1] + sep[2] * sep[2]
                inverse = lax.rsqrt(jnp.maximum(squared, 1e-30))
                inv_sq = inverse * inverse
                factor = (0.75 * radius) * inverse
                cubed = factor * inv_sq
                near = squared < near_sq
                iso = jnp.where(
                    near, 1.0 - (9.0 / 32.0 / radius) * (squared * inverse), factor + (2.0 / 3.0 * radius * radius) * cubed
                )
                dyad = jnp.where(
                    near,
                    (3.0 / 32.0 / radius) * jnp.minimum(inverse, 1000.0 / radius),
                    cubed * (1.0 - (2.0 * radius * radius) * inv_sq),
                )
                pieces.append(jnp.concatenate([dyad * s for s in sep] + [iso], axis=0))
            exact = jnp.concatenate(pieces, axis=1)
            upper = exact.astype(BF16)
            lower = (exact - upper.astype(F32)).astype(BF16)
            tile = weights[p * wide : (p + 1) * wide, :]
            total += jnp.dot(
                jnp.concatenate([upper, lower], axis=1), jnp.concatenate([tile, tile], axis=0), preferred_element_type=F32
            )
        scale = jnp.where(
            which == 0, home[0] - 0.5, jnp.where(which == 1, home[1] - 0.5, jnp.where(which == 2, home[2] - 0.5, -1.0))
        )
        iso_part = total[3 * ROWS :]
        return [
            scale * total[c * ROWS : (c + 1) * ROWS] + jnp.where(which == c, iso_part, 0.0) for c in range(3)
        ]

    def fold(spread, tz):
        sums = []
        for both in spread:
            for shift in (64, 32, 16):
                both = both + pltpu.roll(both, shift, 1)
            sums += [both[8 * b : 8 * b + 8] for b in range(4)]
        first = sums[0]
        for g in range(1, 8):
            first = jnp.where(group == g, sums[g], first)
        second = sums[8]
        for g in range(1, 4):
            second = jnp.where(group % 4 == g, sums[8 + g], second)
        second = jnp.where(lane < 64, second, pltpu.roll(second, 4, 0))
        sent[tz, 0:8] = first
        sent[tz, 8:12] = second[0:4]

    def give(tz):
        @pl.when((tz >= 0) & (tz != z))
        def _():
            send(sent.at[tz], landed.at[z], part_sem, device(x, y, tz, core))

        @pl.when(tz == z)
        def _():
            landed[z] = sent[z]

    def one_target(tz, carry):
        home, spread = carry
        arrived(tz + 1)
        later = columns(jnp.minimum(tz + 1, NZ - 1))
        fold(spread, jnp.maximum(tz - 1, 0))
        spread = pair_sums(home)
        give(tz - 1)
        return later, spread

    arrived(0)
    zeros = [jnp.zeros((ROWS, LANES), F32)] * 3
    _, spread = lax.fori_loop(0, NZ, one_target, (columns(0), zeros))
    fold(spread, NZ - 1)
    give(jnp.int32(NZ - 1))

    wait(landed.at[pl.ds(0, NZ - 1)], part_sem)
    whole = landed[0]
    for k in range(1, NZ):
        whole = whole + landed[k]
    packed = jnp.concatenate([whole, jnp.zeros((LANES - 12, LANES), F32)], axis=0)
    turned = jnp.transpose(packed)
    out_lane = lax.broadcasted_iota(jnp.int32, (HALF, LANES), 1)
    for c in range(3):
        made = jnp.zeros((HALF, LANES), F32)
        for b in range(4):
            if c < 2:
                piece = turned[(c * 4 + b) * HALF : (c * 4 + b + 1) * HALF]
                made = jnp.where(out_lane // 8 == b, pltpu.roll(piece, 8 * b, 1) if b else piece, made)
            else:
                for u in range(2):
                    piece = turned[(u * 4 + b) * HALF : (u * 4 + b + 1) * HALF]
                    shift = (8 * b + 4 * u - 8) % LANES
                    made = jnp.where(out_lane // 4 == 2 * b + u, pltpu.roll(piece, shift, 1) if shift else piece, made)
        out_ref[c] = made[:, 0:ROWS]

    wait(target_row.at[pl.ds(0, 2 * REACH)], send_sem)
    wait(target_row.at[pl.ds(0, 2 * REACH - 1)], send_sem)
    wait(src_row.at[0, pl.ds(0, CHIPS - 1)], send_sem)
    wait(src_row.at[1], send_sem)
    wait(src_block.at[0, pl.ds(0, CHIPS - 1)], send_sem)
    wait(src_block.at[1], send_sem)
    wait(landed.at[pl.ds(0, NZ - 1)], send_sem)


def body(positions, forces):
    total = positions.shape[1] * lax.axis_size("blk") * lax.axis_size("quad")
    radius = radius_scale / total ** (1.0 / 3.0)
    dma = pltpu.SemaphoreType.DMA
    return pl.pallas_call(
        functools.partial(kernel, radius),
        out_shape=jax.ShapeDtypeStruct(forces.shape, F32),
        in_specs=[pl.BlockSpec(memory_space=pltpu.HBM)] * 2,
        out_specs=pl.BlockSpec(memory_space=pltpu.VMEM),
        scratch_shapes=[
            pltpu.VMEM((3, ROWS), F32),
            pltpu.VMEM((3, HALF, ROWS), F32),
            pltpu.VMEM((1, 1, LANES), F32),
            pltpu.VMEM((HALF, LANES), F32),
            pltpu.VMEM((2, CHIPS, 1, LANES), F32),
            pltpu.VMEM((2, CHIPS, HALF, LANES), F32),
            pltpu.VMEM((NZ, 1, LANES), F32),
            pltpu.VMEM((PLANE * ROWS, LANES), BF16),
            pltpu.VMEM((3, 8, PLANE * ROWS), F32),
            pltpu.VMEM((NZ, 12, LANES), F32),
            pltpu.VMEM((NZ, 12, LANES), F32),
            dma((2,)),
            dma,
            dma((NZ,)),
            dma((2,)),
            dma((2,)),
            dma,
            pltpu.SemaphoreType.REGULAR((CHIPS,)),
        ],
        compiler_params=pltpu.CompilerParams(collective_id=0, has_side_effects=True, vmem_limit_bytes=32 * 1024 * 1024),
    )(*(pltpu.with_memory_space_constraint(a, pltpu.HBM) for a in (positions, forces)))


def solution(mesh):
    in_specs = (P(None, ("blk", "quad")), P(None, None, ("blk", "quad")))
    out_specs = P(None, None, ("blk", "quad"))
    return jax.shard_map(body, mesh=mesh, in_specs=in_specs, out_specs=out_specs, check_vma=False)
```

```python
import functools

import jax
import jax.numpy as jnp
from jax import lax
from jax.experimental import pallas as pl
from jax.experimental.pallas import tpu as pltpu
from jax.sharding import PartitionSpec as P

MESH = pl.DeviceIdType.MESH
F32 = jnp.float32
BF16 = jnp.bfloat16

radius_scale = 0.3

NX, NY, NZ = 4, 4, 16
CHIPS = NX * NY
PLANE = CHIPS * 2
REACH = NZ // 4
LANES = 128
ROWS = 32
HALF = ROWS // 2
GROUPS = LANES // HALF
SOON = 12


def place():
    blk, quad = lax.axis_index("blk"), lax.axis_index("quad")
    x = (quad // 2) * 2 + (blk // NZ) % 2
    return x, blk // (2 * NZ), blk % NZ, quad % 2


def device(x, y, z, core):
    return ((y * 2 + x % 2) * NZ + z, (x // 2) * 2 + core)


def slot_of(x, y):
    return (x // 2) * 8 + (y // 2) * 4 + (x % 2) * 2 + y % 2


def slot_device(slot, z, core):
    return device((slot // 8) * 2 + (slot // 2) % 2, ((slot // 4) % 2) * 2 + slot % 2, z, core)


def widened(value):
    return jnp.concatenate([value, jnp.zeros((value.shape[0], LANES - ROWS), F32)], axis=1)


def kernel(radius, pos_hbm, force_hbm, out_ref, pos_in, force_in, my_row, my_block, src_row, src_block, target_row,
           weights, src_pos, sent, landed, in_sem, send_sem, line_sem, row_sem, block_sem, part_sem, open_sem):
    x, y, z, core = place()
    plane_slot = slot_of(x, y)
    sibling = device(x, y, z, 1 - core)
    early = plane_slot < SOON
    met = jnp.where(early, SOON, CHIPS)
    turn = (plane_slot % GROUPS) * HALF
    load_pos = pltpu.make_async_copy(pos_hbm, pos_in, in_sem.at[0])
    load_force = pltpu.make_async_copy(force_hbm, force_in, in_sem.at[1])
    load_pos.start()
    load_force.start()

    def on_line(k):
        return device(x, y, (z + k + NZ) % NZ, core)

    line = [k for d in range(REACH, 0, -1) for k in (d, -d)]
    barrier = pltpu.get_barrier_semaphore()
    for k in line:
        pl.semaphore_signal(barrier, 1, device_id=on_line(k), device_id_type=MESH)
    @pl.loop(jnp.where(early, 0, SOON), CHIPS)
    def _(slot):
        @pl.when(slot != plane_slot)
        def _():
            pl.semaphore_signal(barrier, 1, device_id=slot_device(slot, z, core), device_id_type=MESH)

    pl.semaphore_signal(barrier, 1, device_id=sibling, device_id_type=MESH)

    lane = lax.broadcasted_iota(jnp.int32, (8, LANES), 1)
    sub = lax.broadcasted_iota(jnp.int32, (8, LANES), 0)
    group = lane // HALF

    load_pos.wait()
    mine = [widened(pos_in[e : e + 1, :]) for e in range(3)]
    row = jnp.zeros((1, LANES), F32)
    for h in range(2):
        for e in range(3):
            m = 3 * h + e
            moved = pltpu.roll(mine[e], (HALF * (m - h)) % LANES, 1)
            row = jnp.where(group[0:1] == m, moved, row)
    my_row[0] = pltpu.roll(jnp.broadcast_to(row, (8, LANES)), turn, 1)[0:1]
    load_force.wait()
    parts = [widened(force_in[e]) for e in range(3)]
    dots = sum((mine[e] - 0.5) * parts[e] for e in range(3))
    stack = jnp.concatenate([*parts, dots], axis=0)
    stack = jnp.concatenate([stack, pltpu.roll(stack, LANES - HALF, 1)], axis=0)
    my_block[...] = jnp.transpose(stack)[0:HALF]

    pl.semaphore_wait(barrier, len(line) + met)

    def send(src, dst, sem, where):
        pltpu.make_async_remote_copy(src, dst, send_sem, sem, device_id=where, device_id_type=MESH).start()

    for k in line:
        send(my_row.at[0], target_row.at[z], line_sem.at[z], on_line(k))
    def send_sources(slot):
        send(my_row.at[0], src_row.at[0, plane_slot], row_sem.at[0], slot_device(slot, z, core))
        send(my_block, src_block.at[0, plane_slot], block_sem.at[0], slot_device(slot, z, core))

    @pl.loop(0, met)
    def _(slot):
        @pl.when(jnp.logical_not(early) & (slot < SOON))
        def _():
            pl.semaphore_signal(open_sem.at[plane_slot], 1, device_id=slot_device(slot, z, core), device_id_type=MESH)

        @pl.when(slot != plane_slot)
        def _():
            send_sources(slot)

    src_row[0, plane_slot] = my_row[0]
    src_block[0, plane_slot] = my_block[...]
    target_row[z] = my_row[0]

    def wait(ref, sem):
        pltpu.make_async_copy(ref, ref, sem).wait()

    up, down = (z + REACH) % NZ, (z + NZ - REACH) % NZ
    @pl.loop(met, CHIPS)
    def _(slot):
        pl.semaphore_wait(open_sem.at[slot], 1)
        send_sources(slot)

    wait(target_row.at[up], line_sem.at[up])
    for k in range(REACH, 0, -1):
        send(target_row.at[up], target_row.at[up], line_sem.at[up], on_line(-k))
    wait(target_row.at[down], line_sem.at[down])
    for k in range(REACH - 1, 0, -1):
        send(target_row.at[down], target_row.at[down], line_sem.at[down], on_line(k))

    half_rows = PLANE * HALF
    core_rows = CHIPS * HALF
    left = lax.broadcasted_iota(jnp.int32, (core_rows, LANES), 1) < LANES // 2

    def prepare(i):
        for tile in range(CHIPS // GROUPS):
            rows = jnp.concatenate([src_row[i, tile * GROUPS + k] for k in range(GROUPS)], axis=0)
            for h in range(2):
                for e in range(3):
                    m = 3 * h + e
                    own = jnp.sum(
                        jnp.where((group - sub - m + 2 * GROUPS) % GROUPS == 0, rows, 0.0), axis=0, keepdims=True
                    )
                    at = (h * (PLANE // GROUPS) + i * (CHIPS // GROUPS) + tile) * LANES
                    own = pltpu.roll(jnp.broadcast_to(own, (8, LANES)), (LANES - HALF * m) % LANES, 1)
                    src_pos[e, :, at : at + LANES] = own
        value = src_block[i].reshape(core_rows, LANES)
        high = value.astype(BF16).astype(F32)
        low = value - high
        at = i * core_rows
        weights[at : at + core_rows] = jnp.where(left, high, pltpu.roll(low, LANES // 2, 1)).astype(BF16)
        at = at + half_rows
        weights[at : at + core_rows] = jnp.where(left, pltpu.roll(high, LANES // 2, 1), low).astype(BF16)

    wait(src_row.at[0, pl.ds(0, CHIPS - 1)], row_sem.at[0])
    send(src_row.at[0], src_row.at[1], row_sem.at[1], sibling)
    wait(src_block.at[0, pl.ds(0, CHIPS - 1)], block_sem.at[0])
    send(src_block.at[0], src_block.at[1], block_sem.at[1], sibling)
    prepare(0)
    wait(src_row.at[1], row_sem.at[1])
    wait(src_block.at[1], block_sem.at[1])
    prepare(1)

    wide = 2 * LANES
    near_sq = 4.0 * radius * radius
    lane_group = lax.broadcasted_iota(jnp.int32, (ROWS, LANES), 1) // HALF

    which = lane_group % 4

    def arrived(tz):
        @pl.when((tz < NZ) & (tz != z) & (tz != up) & (tz != down))
        def _():
            wait(target_row.at[tz], line_sem.at[tz])

    def columns(tz):
        theirs = pltpu.roll(jnp.broadcast_to(target_row[tz], (8, LANES)), LANES - turn, 1)
        turned = jnp.transpose(jnp.broadcast_to(theirs[0:1], (LANES, LANES)))
        return [
            jnp.concatenate([turned[e * HALF : (e + 1) * HALF], turned[(3 + e) * HALF : (4 + e) * HALF]], axis=0)
            for e in range(3)
        ]

    def pair_sums(home):
        total = jnp.zeros((4 * ROWS, LANES), F32)
        for p in range(2 * half_rows // wide):
            pieces = []
            for q in range(2):
                at = p * wide + q * LANES
                sep = [
                    (home[e].reshape(ROWS // 8, 8, LANES) - src_pos[e, :, at : at + LANES][None]).reshape(ROWS, LANES)
                    for e in range(3)
                ]
                squared = sep[0] * sep[0] + sep[1] * sep[1] + sep[2] * sep[2]
                inverse = lax.rsqrt(jnp.maximum(squared, 1e-30))
                inv_sq = inverse * inverse
                factor = (0.75 * radius) * inverse
                cubed = factor * inv_sq
                near = squared < near_sq
                iso = jnp.where(
                    near, 1.0 - (9.0 / 32.0 / radius) * (squared * inverse), factor + (2.0 / 3.0 * radius * radius) * cubed
                )
                dyad = jnp.where(
                    near,
                    (3.0 / 32.0 / radius) * jnp.minimum(inverse, 1000.0 / radius),
                    cubed * (1.0 - (2.0 * radius * radius) * inv_sq),
                )
                pieces.append(jnp.concatenate([dyad * s for s in sep] + [iso], axis=0))
            exact = jnp.concatenate(pieces, axis=1)
            upper = exact.astype(BF16)
            lower = (exact - upper.astype(F32)).astype(BF16)
            tile = weights[p * wide : (p + 1) * wide, :]
            total += jnp.dot(
                jnp.concatenate([upper, lower], axis=1), jnp.concatenate([tile, tile], axis=0), preferred_element_type=F32
            )
        scale = jnp.where(
            which == 0, home[0] - 0.5, jnp.where(which == 1, home[1] - 0.5, jnp.where(which == 2, home[2] - 0.5, -1.0))
        )
        iso_part = total[3 * ROWS :]
        return [
            scale * total[c * ROWS : (c + 1) * ROWS] + jnp.where(which == c, iso_part, 0.0) for c in range(3)
        ]

    def fold(spread, tz):
        sums = []
        for both in spread:
            for shift in (64, 32, 16):
                both = both + pltpu.roll(both, shift, 1)
            sums += [both[8 * b : 8 * b + 8] for b in range(4)]
        first = sums[0]
        for g in range(1, 8):
            first = jnp.where(group == g, sums[g], first)
        second = sums[8]
        for g in range(1, 4):
            second = jnp.where(group % 4 == g, sums[8 + g], second)
        second = jnp.where(lane < 64, second, pltpu.roll(second, 4, 0))
        sent[tz, 0:8] = first
        sent[tz, 8:12] = second[0:4]

    def give(tz):
        @pl.when((tz >= 0) & (tz != z))
        def _():
            send(sent.at[tz], landed.at[z], part_sem, device(x, y, tz, core))

        @pl.when(tz == z)
        def _():
            landed[z] = sent[z]

    def one_target(tz, carry):
        home, spread = carry
        arrived(tz + 1)
        later = columns(jnp.minimum(tz + 1, NZ - 1))
        fold(spread, jnp.maximum(tz - 1, 0))
        spread = pair_sums(home)
        give(tz - 1)
        return later, spread

    arrived(0)
    zeros = [jnp.zeros((ROWS, LANES), F32)] * 3
    _, spread = lax.fori_loop(0, NZ, one_target, (columns(0), zeros))
    fold(spread, NZ - 1)
    give(jnp.int32(NZ - 1))

    wait(landed.at[pl.ds(0, NZ - 1)], part_sem)
    whole = landed[0]
    for k in range(1, NZ):
        whole = whole + landed[k]
    packed = jnp.concatenate([whole, jnp.zeros((LANES - 12, LANES), F32)], axis=0)
    turned = jnp.transpose(packed)
    out_lane = lax.broadcasted_iota(jnp.int32, (HALF, LANES), 1)
    for c in range(3):
        made = jnp.zeros((HALF, LANES), F32)
        for b in range(4):
            if c < 2:
                piece = turned[(c * 4 + b) * HALF : (c * 4 + b + 1) * HALF]
                made = jnp.where(out_lane // 8 == b, pltpu.roll(piece, 8 * b, 1) if b else piece, made)
            else:
                for u in range(2):
                    piece = turned[(u * 4 + b) * HALF : (u * 4 + b + 1) * HALF]
                    shift = (8 * b + 4 * u - 8) % LANES
                    made = jnp.where(out_lane // 4 == 2 * b + u, pltpu.roll(piece, shift, 1) if shift else piece, made)
        out_ref[c] = made[:, 0:ROWS]

    wait(target_row.at[pl.ds(0, 2 * REACH)], send_sem)
    wait(target_row.at[pl.ds(0, 2 * REACH - 1)], send_sem)
    wait(src_row.at[0, pl.ds(0, CHIPS - 1)], send_sem)
    wait(src_row.at[1], send_sem)
    wait(src_block.at[0, pl.ds(0, CHIPS - 1)], send_sem)
    wait(src_block.at[1], send_sem)
    wait(landed.at[pl.ds(0, NZ - 1)], send_sem)


def body(positions, forces):
    total = positions.shape[1] * lax.axis_size("blk") * lax.axis_size("quad")
    radius = radius_scale / total ** (1.0 / 3.0)
    dma = pltpu.SemaphoreType.DMA
    return pl.pallas_call(
        functools.partial(kernel, radius),
        out_shape=jax.ShapeDtypeStruct(forces.shape, F32),
        in_specs=[pl.BlockSpec(memory_space=pltpu.HBM)] * 2,
        out_specs=pl.BlockSpec(memory_space=pltpu.VMEM),
        scratch_shapes=[
            pltpu.VMEM((3, ROWS), F32),
            pltpu.VMEM((3, HALF, ROWS), F32),
            pltpu.VMEM((1, 1, LANES), F32),
            pltpu.VMEM((HALF, LANES), F32),
            pltpu.VMEM((2, CHIPS, 1, LANES), F32),
            pltpu.VMEM((2, CHIPS, HALF, LANES), F32),
            pltpu.VMEM((NZ, 1, LANES), F32),
            pltpu.VMEM((PLANE * ROWS, LANES), BF16),
            pltpu.VMEM((3, 8, PLANE * ROWS), F32),
            pltpu.VMEM((NZ, 12, LANES), F32),
            pltpu.VMEM((NZ, 12, LANES), F32),
            dma((2,)),
            dma,
            dma((NZ,)),
            dma((2,)),
            dma((2,)),
            dma,
            pltpu.SemaphoreType.REGULAR((CHIPS,)),
        ],
        compiler_params=pltpu.CompilerParams(collective_id=0, has_side_effects=True, vmem_limit_bytes=32 * 1024 * 1024),
    )(*(pltpu.with_memory_space_constraint(a, pltpu.HBM) for a in (positions, forces)))


def solution(mesh):
    in_specs = (P(None, ("blk", "quad")), P(None, None, ("blk", "quad")))
    out_specs = P(None, None, ("blk", "quad"))
    return jax.shard_map(body, mesh=mesh, in_specs=in_specs, out_specs=out_specs, check_vma=False)
```

```python
import functools

import jax
import jax.numpy as jnp
from jax import lax
from jax.experimental import pallas as pl
from jax.experimental.pallas import tpu as pltpu
from jax.sharding import PartitionSpec as P

MESH = pl.DeviceIdType.MESH
F32 = jnp.float32
BF16 = jnp.bfloat16

radius_scale = 0.3

NX, NY, NZ = 4, 4, 16
CHIPS = NX * NY
PLANE = CHIPS * 2
REACH = NZ // 4
LANES = 128
ROWS = 32
HALF = ROWS // 2
GROUPS = LANES // HALF
SOON = 12


def place():
    blk, quad = lax.axis_index("blk"), lax.axis_index("quad")
    x = (quad // 2) * 2 + (blk // NZ) % 2
    return x, blk // (2 * NZ), blk % NZ, quad % 2


def device(x, y, z, core):
    return ((y * 2 + x % 2) * NZ + z, (x // 2) * 2 + core)


def slot_of(x, y):
    return (x // 2) * 8 + (y // 2) * 4 + (x % 2) * 2 + y % 2


def slot_device(slot, z, core):
    return device((slot // 8) * 2 + (slot // 2) % 2, ((slot // 4) % 2) * 2 + slot % 2, z, core)


def widened(value):
    return jnp.concatenate([value, jnp.zeros((value.shape[0], LANES - ROWS), F32)], axis=1)


def kernel(radius, pos_hbm, force_hbm, out_ref, pos_in, force_in, my_row, my_block, src_row, src_block, target_row,
           weights, src_pos, sent, landed, in_sem, send_sem, line_sem, row_sem, block_sem, part_sem, open_sem):
    x, y, z, core = place()
    plane_slot = slot_of(x, y)
    sibling = device(x, y, z, 1 - core)
    early = plane_slot < SOON
    met = jnp.where(early, SOON, CHIPS)
    turn = (plane_slot % GROUPS) * HALF
    load_pos = pltpu.make_async_copy(pos_hbm, pos_in, in_sem.at[0])
    load_force = pltpu.make_async_copy(force_hbm, force_in, in_sem.at[1])
    load_pos.start()
    load_force.start()

    def on_line(k):
        return device(x, y, (z + k + NZ) % NZ, core)

    line = [k for d in range(REACH, 0, -1) for k in (d, -d)]
    barrier = pltpu.get_barrier_semaphore()
    for k in line:
        pl.semaphore_signal(barrier, 1, device_id=on_line(k), device_id_type=MESH)
    @pl.loop(jnp.where(early, 0, SOON), CHIPS)
    def _(slot):
        @pl.when(slot != plane_slot)
        def _():
            pl.semaphore_signal(barrier, 1, device_id=slot_device(slot, z, core), device_id_type=MESH)

    pl.semaphore_signal(barrier, 1, device_id=sibling, device_id_type=MESH)

    lane = lax.broadcasted_iota(jnp.int32, (8, LANES), 1)
    sub = lax.broadcasted_iota(jnp.int32, (8, LANES), 0)
    group = lane // HALF

    load_pos.wait()
    mine = [widened(pos_in[e : e + 1, :]) for e in range(3)]
    row = jnp.zeros((1, LANES), F32)
    for h in range(2):
        for e in range(3):
            m = 3 * h + e
            moved = pltpu.roll(mine[e], (HALF * (m - h)) % LANES, 1)
            row = jnp.where(group[0:1] == m, moved, row)
    my_row[0] = pltpu.roll(jnp.broadcast_to(row, (8, LANES)), turn, 1)[0:1]
    load_force.wait()
    parts = [widened(force_in[e]) for e in range(3)]
    dots = sum((mine[e] - 0.5) * parts[e] for e in range(3))
    stack = jnp.concatenate([*parts, dots], axis=0)
    stack = jnp.concatenate([stack, pltpu.roll(stack, LANES - HALF, 1)], axis=0)
    my_block[...] = jnp.transpose(stack)[0:HALF]

    pl.semaphore_wait(barrier, len(line) + met)

    def send(src, dst, sem, where):
        pltpu.make_async_remote_copy(src, dst, send_sem, sem, device_id=where, device_id_type=MESH).start()

    for k in line:
        send(my_row.at[0], target_row.at[z], line_sem.at[z], on_line(k))
    def send_sources(slot):
        send(my_row.at[0], src_row.at[0, plane_slot], row_sem.at[0], slot_device(slot, z, core))
        send(my_block, src_block.at[0, plane_slot], block_sem.at[0], slot_device(slot, z, core))

    @pl.loop(0, met)
    def _(slot):
        @pl.when(jnp.logical_not(early) & (slot < SOON))
        def _():
            pl.semaphore_signal(open_sem.at[plane_slot], 1, device_id=slot_device(slot, z, core), device_id_type=MESH)

        @pl.when(slot != plane_slot)
        def _():
            send_sources(slot)

    src_row[0, plane_slot] = my_row[0]
    src_block[0, plane_slot] = my_block[...]
    target_row[z] = my_row[0]

    def wait(ref, sem):
        pltpu.make_async_copy(ref, ref, sem).wait()

    up, down = (z + REACH) % NZ, (z + NZ - REACH) % NZ
    wait(target_row.at[up], line_sem.at[up])
    for k in range(REACH, 0, -1):
        send(target_row.at[up], target_row.at[up], line_sem.at[up], on_line(-k))
    wait(target_row.at[down], line_sem.at[down])
    for k in range(REACH - 1, 0, -1):
        send(target_row.at[down], target_row.at[down], line_sem.at[down], on_line(k))

    @pl.loop(met, CHIPS)
    def _(slot):
        pl.semaphore_wait(open_sem.at[slot], 1)
        send_sources(slot)

    half_rows = PLANE * HALF
    core_rows = CHIPS * HALF
    left = lax.broadcasted_iota(jnp.int32, (core_rows, LANES), 1) < LANES // 2

    def prepare(i):
        for tile in range(CHIPS // GROUPS):
            rows = jnp.concatenate([src_row[i, tile * GROUPS + k] for k in range(GROUPS)], axis=0)
            for h in range(2):
                for e in range(3):
                    m = 3 * h + e
                    own = jnp.sum(
                        jnp.where((group - sub - m + 2 * GROUPS) % GROUPS == 0, rows, 0.0), axis=0, keepdims=True
                    )
                    at = (h * (PLANE // GROUPS) + i * (CHIPS // GROUPS) + tile) * LANES
                    own = pltpu.roll(jnp.broadcast_to(own, (8, LANES)), (LANES - HALF * m) % LANES, 1)
                    src_pos[e, :, at : at + LANES] = own
        value = src_block[i].reshape(core_rows, LANES)
        high = value.astype(BF16).astype(F32)
        low = value - high
        at = i * core_rows
        weights[at : at + core_rows] = jnp.where(left, high, pltpu.roll(low, LANES // 2, 1)).astype(BF16)
        at = at + half_rows
        weights[at : at + core_rows] = jnp.where(left, pltpu.roll(high, LANES // 2, 1), low).astype(BF16)

    wait(src_row.at[0, pl.ds(0, CHIPS - 1)], row_sem.at[0])
    send(src_row.at[0], src_row.at[1], row_sem.at[1], sibling)
    wait(src_block.at[0, pl.ds(0, CHIPS - 1)], block_sem.at[0])
    send(src_block.at[0], src_block.at[1], block_sem.at[1], sibling)
    prepare(0)
    wait(src_row.at[1], row_sem.at[1])
    wait(src_block.at[1], block_sem.at[1])
    prepare(1)

    wide = 2 * LANES
    near_sq = 4.0 * radius * radius
    lane_group = lax.broadcasted_iota(jnp.int32, (ROWS, LANES), 1) // HALF

    which = lane_group % 4

    def arrived(tz):
        @pl.when((tz < NZ) & (tz != z) & (tz != up) & (tz != down))
        def _():
            wait(target_row.at[tz], line_sem.at[tz])

    def columns(tz):
        theirs = pltpu.roll(jnp.broadcast_to(target_row[tz], (8, LANES)), LANES - turn, 1)
        turned = jnp.broadcast_to(jnp.transpose(theirs)[:, 0:1], (LANES, LANES))
        return [
            jnp.concatenate([turned[e * HALF : (e + 1) * HALF], turned[(3 + e) * HALF : (4 + e) * HALF]], axis=0)
            for e in range(3)
        ]

    def pair_sums(home):
        total = jnp.zeros((4 * ROWS, LANES), F32)
        for p in range(2 * half_rows // wide):
            pieces = []
            for q in range(2):
                at = p * wide + q * LANES
                sep = [
                    (home[e].reshape(ROWS // 8, 8, LANES) - src_pos[e, :, at : at + LANES][None]).reshape(ROWS, LANES)
                    for e in range(3)
                ]
                squared = sep[0] * sep[0] + sep[1] * sep[1] + sep[2] * sep[2]
                inverse = lax.rsqrt(jnp.maximum(squared, 1e-30))
                inv_sq = inverse * inverse
                factor = (0.75 * radius) * inverse
                cubed = factor * inv_sq
                near = squared < near_sq
                iso = jnp.where(
                    near, 1.0 - (9.0 / 32.0 / radius) * (squared * inverse), factor + (2.0 / 3.0 * radius * radius) * cubed
                )
                dyad = jnp.where(
                    near,
                    (3.0 / 32.0 / radius) * jnp.minimum(inverse, 1000.0 / radius),
                    cubed * (1.0 - (2.0 * radius * radius) * inv_sq),
                )
                pieces.append(jnp.concatenate([dyad * s for s in sep] + [iso], axis=0))
            exact = jnp.concatenate(pieces, axis=1)
            upper = exact.astype(BF16)
            lower = (exact - upper.astype(F32)).astype(BF16)
            tile = weights[p * wide : (p + 1) * wide, :]
            total += jnp.dot(
                jnp.concatenate([upper, lower], axis=1), jnp.concatenate([tile, tile], axis=0), preferred_element_type=F32
            )
        scale = jnp.where(
            which == 0, home[0] - 0.5, jnp.where(which == 1, home[1] - 0.5, jnp.where(which == 2, home[2] - 0.5, -1.0))
        )
        iso_part = total[3 * ROWS :]
        return [
            scale * total[c * ROWS : (c + 1) * ROWS] + jnp.where(which == c, iso_part, 0.0) for c in range(3)
        ]

    def fold(spread, tz):
        sums = []
        for both in spread:
            for shift in (64, 32, 16):
                both = both + pltpu.roll(both, shift, 1)
            sums += [both[8 * b : 8 * b + 8] for b in range(4)]
        first = sums[0]
        for g in range(1, 8):
            first = jnp.where(group == g, sums[g], first)
        second = sums[8]
        for g in range(1, 4):
            second = jnp.where(group % 4 == g, sums[8 + g], second)
        second = jnp.where(lane < 64, second, pltpu.roll(second, 4, 0))
        sent[tz, 0:8] = first
        sent[tz, 8:12] = second[0:4]

    def give(tz):
        @pl.when((tz >= 0) & (tz != z))
        def _():
            send(sent.at[tz], landed.at[z], part_sem, device(x, y, tz, core))

        @pl.when(tz == z)
        def _():
            landed[z] = sent[z]

    def one_target(tz, carry):
        home, spread = carry
        arrived(tz + 1)
        later = columns(jnp.minimum(tz + 1, NZ - 1))
        fold(spread, jnp.maximum(tz - 1, 0))
        spread = pair_sums(home)
        give(tz - 1)
        return later, spread

    arrived(0)
    zeros = [jnp.zeros((ROWS, LANES), F32)] * 3
    _, spread = lax.fori_loop(0, NZ, one_target, (columns(0), zeros))
    fold(spread, NZ - 1)
    give(jnp.int32(NZ - 1))

    wait(landed.at[pl.ds(0, NZ - 1)], part_sem)
    whole = landed[0]
    for k in range(1, NZ):
        whole = whole + landed[k]
    packed = jnp.concatenate([whole, jnp.zeros((LANES - 12, LANES), F32)], axis=0)
    turned = jnp.transpose(packed)
    out_lane = lax.broadcasted_iota(jnp.int32, (HALF, LANES), 1)
    for c in range(3):
        made = jnp.zeros((HALF, LANES), F32)
        for b in range(4):
            if c < 2:
                piece = turned[(c * 4 + b) * HALF : (c * 4 + b + 1) * HALF]
                made = jnp.where(out_lane // 8 == b, pltpu.roll(piece, 8 * b, 1) if b else piece, made)
            else:
                for u in range(2):
                    piece = turned[(u * 4 + b) * HALF : (u * 4 + b + 1) * HALF]
                    shift = (8 * b + 4 * u - 8) % LANES
                    made = jnp.where(out_lane // 4 == 2 * b + u, pltpu.roll(piece, shift, 1) if shift else piece, made)
        out_ref[c] = made[:, 0:ROWS]

    wait(target_row.at[pl.ds(0, 2 * REACH)], send_sem)
    wait(target_row.at[pl.ds(0, 2 * REACH - 1)], send_sem)
    wait(src_row.at[0, pl.ds(0, CHIPS - 1)], send_sem)
    wait(src_row.at[1], send_sem)
    wait(src_block.at[0, pl.ds(0, CHIPS - 1)], send_sem)
    wait(src_block.at[1], send_sem)
    wait(landed.at[pl.ds(0, NZ - 1)], send_sem)


def body(positions, forces):
    total = positions.shape[1] * lax.axis_size("blk") * lax.axis_size("quad")
    radius = radius_scale / total ** (1.0 / 3.0)
    dma = pltpu.SemaphoreType.DMA
    return pl.pallas_call(
        functools.partial(kernel, radius),
        out_shape=jax.ShapeDtypeStruct(forces.shape, F32),
        in_specs=[pl.BlockSpec(memory_space=pltpu.HBM)] * 2,
        out_specs=pl.BlockSpec(memory_space=pltpu.VMEM),
        scratch_shapes=[
            pltpu.VMEM((3, ROWS), F32),
            pltpu.VMEM((3, HALF, ROWS), F32),
            pltpu.VMEM((1, 1, LANES), F32),
            pltpu.VMEM((HALF, LANES), F32),
            pltpu.VMEM((2, CHIPS, 1, LANES), F32),
            pltpu.VMEM((2, CHIPS, HALF, LANES), F32),
            pltpu.VMEM((NZ, 1, LANES), F32),
            pltpu.VMEM((PLANE * ROWS, LANES), BF16),
            pltpu.VMEM((3, 8, PLANE * ROWS), F32),
            pltpu.VMEM((NZ, 12, LANES), F32),
            pltpu.VMEM((NZ, 12, LANES), F32),
            dma((2,)),
            dma,
            dma((NZ,)),
            dma((2,)),
            dma((2,)),
            dma,
            pltpu.SemaphoreType.REGULAR((CHIPS,)),
        ],
        compiler_params=pltpu.CompilerParams(collective_id=0, has_side_effects=True, vmem_limit_bytes=32 * 1024 * 1024),
    )(*(pltpu.with_memory_space_constraint(a, pltpu.HBM) for a in (positions, forces)))


def solution(mesh):
    in_specs = (P(None, ("blk", "quad")), P(None, None, ("blk", "quad")))
    out_specs = P(None, None, ("blk", "quad"))
    return jax.shard_map(body, mesh=mesh, in_specs=in_specs, out_specs=out_specs, check_vma=False)
```

```python
import functools

import jax
import jax.numpy as jnp
from jax import lax
from jax.experimental import pallas as pl
from jax.experimental.pallas import tpu as pltpu
from jax.sharding import PartitionSpec as P

MESH = pl.DeviceIdType.MESH
F32 = jnp.float32
BF16 = jnp.bfloat16

radius_scale = 0.3

NX, NY, NZ = 4, 4, 16
CHIPS = NX * NY
PLANE = CHIPS * 2
REACH = NZ // 4
LANES = 128
ROWS = 32
HALF = ROWS // 2
GROUPS = LANES // HALF
SOON = 12


def place():
    blk, quad = lax.axis_index("blk"), lax.axis_index("quad")
    x = (quad // 2) * 2 + (blk // NZ) % 2
    return x, blk // (2 * NZ), blk % NZ, quad % 2


def device(x, y, z, core):
    return ((y * 2 + x % 2) * NZ + z, (x // 2) * 2 + core)


def slot_of(x, y):
    return (x // 2) * 8 + (y // 2) * 4 + (x % 2) * 2 + y % 2


def slot_device(slot, z, core):
    return device((slot // 8) * 2 + (slot // 2) % 2, ((slot // 4) % 2) * 2 + slot % 2, z, core)


def widened(value):
    return jnp.concatenate([value, jnp.zeros((value.shape[0], LANES - ROWS), F32)], axis=1)


def kernel(radius, pos_hbm, force_hbm, out_ref, pos_in, force_in, my_row, my_block, src_row, src_block, target_row,
           weights, src_pos, sent, landed, in_sem, send_sem, line_sem, row_sem, block_sem, part_sem, open_sem):
    x, y, z, core = place()
    plane_slot = slot_of(x, y)
    sibling = device(x, y, z, 1 - core)
    early = plane_slot < SOON
    met = jnp.where(early, SOON, CHIPS)
    turn = (plane_slot % GROUPS) * HALF
    load_pos = pltpu.make_async_copy(pos_hbm, pos_in, in_sem.at[0])
    load_force = pltpu.make_async_copy(force_hbm, force_in, in_sem.at[1])
    load_pos.start()
    load_force.start()

    def on_line(k):
        return device(x, y, (z + k + NZ) % NZ, core)

    line = [k for d in range(REACH, 0, -1) for k in (d, -d)]
    barrier = pltpu.get_barrier_semaphore()
    for k in line:
        pl.semaphore_signal(barrier, 1, device_id=on_line(k), device_id_type=MESH)
    @pl.loop(jnp.where(early, 0, SOON), CHIPS)
    def _(slot):
        @pl.when(slot != plane_slot)
        def _():
            pl.semaphore_signal(barrier, 1, device_id=slot_device(slot, z, core), device_id_type=MESH)

    pl.semaphore_signal(barrier, 1, device_id=sibling, device_id_type=MESH)

    lane = lax.broadcasted_iota(jnp.int32, (8, LANES), 1)
    sub = lax.broadcasted_iota(jnp.int32, (8, LANES), 0)
    group = lane // HALF

    load_pos.wait()
    mine = [widened(pos_in[e : e + 1, :]) for e in range(3)]
    row = jnp.zeros((1, LANES), F32)
    for h in range(2):
        for e in range(3):
            m = 3 * h + e
            moved = pltpu.roll(mine[e], (HALF * (m - h)) % LANES, 1)
            row = jnp.where(group[0:1] == m, moved, row)
    my_row[0] = pltpu.roll(jnp.broadcast_to(row, (8, LANES)), turn, 1)[0:1]
    load_force.wait()
    parts = [widened(force_in[e]) for e in range(3)]
    dots = sum((mine[e] - 0.5) * parts[e] for e in range(3))
    stack = jnp.concatenate([*parts, dots], axis=0)
    stack = jnp.concatenate([stack, pltpu.roll(stack, LANES - HALF, 1)], axis=0)
    my_block[...] = jnp.transpose(stack)[0:HALF]

    pl.semaphore_wait(barrier, len(line) + met)

    def send(src, dst, sem, where):
        pltpu.make_async_remote_copy(src, dst, send_sem, sem, device_id=where, device_id_type=MESH).start()

    for k in line:
        send(my_row.at[0], target_row.at[z], line_sem.at[z], on_line(k))
    def send_sources(slot):
        send(my_row.at[0], src_row.at[0, plane_slot], row_sem.at[0], slot_device(slot, z, core))
        send(my_block, src_block.at[0, plane_slot], block_sem.at[0], slot_device(slot, z, core))

    @pl.loop(0, met)
    def _(slot):
        @pl.when(jnp.logical_not(early) & (slot < SOON))
        def _():
            pl.semaphore_signal(open_sem.at[plane_slot], 1, device_id=slot_device(slot, z, core), device_id_type=MESH)

        @pl.when(slot != plane_slot)
        def _():
            send_sources(slot)

    src_row[0, plane_slot] = my_row[0]
    src_block[0, plane_slot] = my_block[...]
    target_row[z] = my_row[0]

    def wait(ref, sem):
        pltpu.make_async_copy(ref, ref, sem).wait()

    up, down = (z + REACH) % NZ, (z + NZ - REACH) % NZ
    @pl.loop(met, CHIPS)
    def _(slot):
        pl.semaphore_wait(open_sem.at[slot], 1)
        send_sources(slot)

    wait(target_row.at[up], line_sem.at[up])
    for k in range(REACH, 0, -1):
        send(target_row.at[up], target_row.at[up], line_sem.at[up], on_line(-k))
    wait(target_row.at[down], line_sem.at[down])
    for k in range(REACH - 1, 0, -1):
        send(target_row.at[down], target_row.at[down], line_sem.at[down], on_line(k))

    half_rows = PLANE * HALF
    core_rows = CHIPS * HALF
    left = lax.broadcasted_iota(jnp.int32, (core_rows, LANES), 1) < LANES // 2

    def prepare(i):
        for tile in range(CHIPS // GROUPS):
            rows = jnp.concatenate([src_row[i, tile * GROUPS + k] for k in range(GROUPS)], axis=0)
            for h in range(2):
                for e in range(3):
                    m = 3 * h + e
                    own = jnp.sum(
                        jnp.where((group - sub - m + 2 * GROUPS) % GROUPS == 0, rows, 0.0), axis=0, keepdims=True
                    )
                    at = (h * (PLANE // GROUPS) + i * (CHIPS // GROUPS) + tile) * LANES
                    own = pltpu.roll(jnp.broadcast_to(own, (8, LANES)), (LANES - HALF * m) % LANES, 1)
                    src_pos[e, :, at : at + LANES] = own
        value = src_block[i].reshape(core_rows, LANES)
        high = value.astype(BF16).astype(F32)
        low = value - high
        at = i * core_rows
        weights[at : at + core_rows] = jnp.where(left, high, pltpu.roll(low, LANES // 2, 1)).astype(BF16)
        at = at + half_rows
        weights[at : at + core_rows] = jnp.where(left, pltpu.roll(high, LANES // 2, 1), low).astype(BF16)

    wait(src_row.at[0, pl.ds(0, CHIPS - 1)], row_sem.at[0])
    send(src_row.at[0], src_row.at[1], row_sem.at[1], sibling)
    wait(src_block.at[0, pl.ds(0, CHIPS - 1)], block_sem.at[0])
    send(src_block.at[0], src_block.at[1], block_sem.at[1], sibling)
    prepare(0)
    wait(src_row.at[1], row_sem.at[1])
    wait(src_block.at[1], block_sem.at[1])
    prepare(1)

    wide = 2 * LANES
    near_sq = 4.0 * radius * radius
    lane_group = lax.broadcasted_iota(jnp.int32, (ROWS, LANES), 1) // HALF

    which = lane_group % 4

    def arrived(tz):
        @pl.when((tz < NZ) & (tz != z) & (tz != up) & (tz != down))
        def _():
            wait(target_row.at[tz], line_sem.at[tz])

    def columns(tz):
        theirs = pltpu.roll(jnp.broadcast_to(target_row[tz], (8, LANES)), LANES - turn, 1)
        turned = jnp.broadcast_to(jnp.transpose(theirs)[:, 0:1], (LANES, LANES))
        return [
            jnp.concatenate([turned[e * HALF : (e + 1) * HALF], turned[(3 + e) * HALF : (4 + e) * HALF]], axis=0)
            for e in range(3)
        ]

    def pair_sums(home):
        total = jnp.zeros((4 * ROWS, LANES), F32)
        for p in range(2 * half_rows // wide):
            pieces = []
            for q in range(2):
                at = p * wide + q * LANES
                sep = [
                    (home[e].reshape(ROWS // 8, 8, LANES) - src_pos[e, :, at : at + LANES][None]).reshape(ROWS, LANES)
                    for e in range(3)
                ]
                squared = sep[0] * sep[0] + sep[1] * sep[1] + sep[2] * sep[2]
                inverse = lax.rsqrt(jnp.maximum(squared, 1e-30))
                inv_sq = inverse * inverse
                factor = (0.75 * radius) * inverse
                cubed = factor * inv_sq
                near = squared < near_sq
                iso = jnp.where(
                    near, 1.0 - (9.0 / 32.0 / radius) * (squared * inverse), factor + (2.0 / 3.0 * radius * radius) * cubed
                )
                dyad = jnp.where(
                    near,
                    (3.0 / 32.0 / radius) * jnp.minimum(inverse, 1000.0 / radius),
                    cubed * (1.0 - (2.0 * radius * radius) * inv_sq),
                )
                pieces.append(jnp.concatenate([dyad * s for s in sep] + [iso], axis=0))
            exact = jnp.concatenate(pieces, axis=1)
            upper = exact.astype(BF16)
            lower = (exact - upper.astype(F32)).astype(BF16)
            tile = weights[p * wide : (p + 1) * wide, :]
            total += jnp.dot(
                jnp.concatenate([upper, lower], axis=1), jnp.concatenate([tile, tile], axis=0), preferred_element_type=F32
            )
        scale = jnp.where(
            which == 0, home[0] - 0.5, jnp.where(which == 1, home[1] - 0.5, jnp.where(which == 2, home[2] - 0.5, -1.0))
        )
        iso_part = total[3 * ROWS :]
        return [
            scale * total[c * ROWS : (c + 1) * ROWS] + jnp.where(which == c, iso_part, 0.0) for c in range(3)
        ]

    def fold(spread, tz):
        sums = []
        for both in spread:
            for shift in (64, 32, 16):
                both = both + pltpu.roll(both, shift, 1)
            sums += [both[8 * b : 8 * b + 8] for b in range(4)]
        first = sums[0]
        for g in range(1, 8):
            first = jnp.where(group == g, sums[g], first)
        second = sums[8]
        for g in range(1, 4):
            second = jnp.where(group % 4 == g, sums[8 + g], second)
        second = jnp.where(lane < 64, second, pltpu.roll(second, 4, 0))
        sent[tz, 0:8] = first
        sent[tz, 8:12] = second[0:4]

    def give(tz):
        @pl.when((tz >= 0) & (tz != z))
        def _():
            send(sent.at[tz], landed.at[z], part_sem, device(x, y, tz, core))

        @pl.when(tz == z)
        def _():
            landed[z] = sent[z]

    def one_target(tz, carry):
        home, spread = carry
        arrived(tz + 1)
        later = columns(jnp.minimum(tz + 1, NZ - 1))
        fold(spread, jnp.maximum(tz - 1, 0))
        spread = pair_sums(home)
        give(tz - 1)
        return later, spread

    arrived(0)
    zeros = [jnp.zeros((ROWS, LANES), F32)] * 3
    _, spread = lax.fori_loop(0, NZ, one_target, (columns(0), zeros))
    fold(spread, NZ - 1)
    give(jnp.int32(NZ - 1))

    wait(landed.at[pl.ds(0, NZ - 1)], part_sem)
    whole = landed[0]
    for k in range(1, NZ):
        whole = whole + landed[k]
    packed = jnp.concatenate([whole, jnp.zeros((LANES - 12, LANES), F32)], axis=0)
    turned = jnp.transpose(packed)
    out_lane = lax.broadcasted_iota(jnp.int32, (HALF, LANES), 1)
    for c in range(3):
        made = jnp.zeros((HALF, LANES), F32)
        for b in range(4):
            if c < 2:
                piece = turned[(c * 4 + b) * HALF : (c * 4 + b + 1) * HALF]
                made = jnp.where(out_lane // 8 == b, pltpu.roll(piece, 8 * b, 1) if b else piece, made)
            else:
                for u in range(2):
                    piece = turned[(u * 4 + b) * HALF : (u * 4 + b + 1) * HALF]
                    shift = (8 * b + 4 * u - 8) % LANES
                    made = jnp.where(out_lane // 4 == 2 * b + u, pltpu.roll(piece, shift, 1) if shift else piece, made)
        out_ref[c] = made[:, 0:ROWS]

    wait(target_row.at[pl.ds(0, 2 * REACH)], send_sem)
    wait(target_row.at[pl.ds(0, 2 * REACH - 1)], send_sem)
    wait(src_row.at[0, pl.ds(0, CHIPS - 1)], send_sem)
    wait(src_row.at[1], send_sem)
    wait(src_block.at[0, pl.ds(0, CHIPS - 1)], send_sem)
    wait(src_block.at[1], send_sem)
    wait(landed.at[pl.ds(0, NZ - 1)], send_sem)


def body(positions, forces):
    total = positions.shape[1] * lax.axis_size("blk") * lax.axis_size("quad")
    radius = radius_scale / total ** (1.0 / 3.0)
    dma = pltpu.SemaphoreType.DMA
    return pl.pallas_call(
        functools.partial(kernel, radius),
        out_shape=jax.ShapeDtypeStruct(forces.shape, F32),
        in_specs=[pl.BlockSpec(memory_space=pltpu.HBM)] * 2,
        out_specs=pl.BlockSpec(memory_space=pltpu.VMEM),
        scratch_shapes=[
            pltpu.VMEM((3, ROWS), F32),
            pltpu.VMEM((3, HALF, ROWS), F32),
            pltpu.VMEM((1, 1, LANES), F32),
            pltpu.VMEM((HALF, LANES), F32),
            pltpu.VMEM((2, CHIPS, 1, LANES), F32),
            pltpu.VMEM((2, CHIPS, HALF, LANES), F32),
            pltpu.VMEM((NZ, 1, LANES), F32),
            pltpu.VMEM((PLANE * ROWS, LANES), BF16),
            pltpu.VMEM((3, 8, PLANE * ROWS), F32),
            pltpu.VMEM((NZ, 12, LANES), F32),
            pltpu.VMEM((NZ, 12, LANES), F32),
            dma((2,)),
            dma,
            dma((NZ,)),
            dma((2,)),
            dma((2,)),
            dma,
            pltpu.SemaphoreType.REGULAR((CHIPS,)),
        ],
        compiler_params=pltpu.CompilerParams(collective_id=0, has_side_effects=True, vmem_limit_bytes=32 * 1024 * 1024),
    )(*(pltpu.with_memory_space_constraint(a, pltpu.HBM) for a in (positions, forces)))


def solution(mesh):
    in_specs = (P(None, ("blk", "quad")), P(None, None, ("blk", "quad")))
    out_specs = P(None, None, ("blk", "quad"))
    return jax.shard_map(body, mesh=mesh, in_specs=in_specs, out_specs=out_specs, check_vma=False)
```
